32 devices in a mesh: gx: 8 (over z, y), gy: 4 (over x, core).
Axes of the slice: x: 2, y: 2, z: 4, core: 2. Of those that a mesh axis runs over, the one named last changes fastest.
Arguments:
- tracers: float32 [4, 8, 512, 1024], P(None, None, 'gy', 'gx'), may hold values from -6 to 6
- velocity: float32 [2, 8, 512, 1024], P(None, None, 'gy', 'gx'), may hold values from -0.35 to 0.35
- mixing: float32 [8, 512, 1024], P(None, 'gy', 'gx'), may hold values from 0.01 to 0.075
- land_mask: int32 [512, 1024], P('gy', 'gx'), may hold values 0 or 1
- remap_weights: bfloat16 [512, 4, 1024, 128], P('gy', None, 'gx'), may hold values from 0 to 0.015625
- remap_dest: int32 [512, 8, 4], P('gy', 'gx'), may hold values from 0 to 511, as said below
Outputs:
- final_tracers: float32 [4, 8, 512, 1024], P(None, None, 'gy', 'gx')
- atmo_fields: float32 [512, 5, 128], P(('gx', 'gy'))
The draws below stay inside these ranges and needn't reach their ends.
Inputs may be any that keep to these rules, and one draw needn't show every extreme that they name: `remap_dest`: block b belongs to owner b // 16; owner o is the device with gx index o // 4 and gy index o % 4 (the order of the output's split over (gx, gy)). Among the 512 entries of one tile (one index of gy and of gx) no owner is named more than 32 times; 4 owners are named exactly 32 times by every tile.
All inputs are finite; a program needn't handle non-finite values. No bound on the sum of `land_mask` on one device may be relied on, other than what follows from the above.
Results may differ from the reference program's by a relative error of at most 0.0003.
Values sent between devices are 32-bit elements; how exact they have to be, the bound alone decides.
No kernel may reach another device: no remote copies, remote signals or barrier semaphores. Data moves between devices by JAX's collectives and lax.ppermute only.
A program may use at most 128 MiB of HBM per device.

```python
import math
import jax
import jax.numpy as jnp
from jax import lax

NTR = 4
LEV = 8
STEPS = 4
CLAT = 128
CLON = 128
KB = 4
NLAT = 512
NLON = 1024
NTILE = 8
OWNERS = 32
ABD = 16
ATB = 512
CAP = 32
HOT = 4


def draw_remap_dest(key, part):
    pairs = CLAT * KB
    hot_key, tile_keys = jax.random.split(jax.random.fold_in(key, 7))
    chosen = jax.random.permutation(hot_key, OWNERS)[:HOT]
    is_hot = jnp.any(jnp.arange(OWNERS)[:, None] == chosen[None, :], axis=1).astype(jnp.int32)

    def one_tile(tile_key):
        score_key, order_key, local_key = jax.random.split(tile_key, 3)
        scores = jax.random.randint(score_key, (OWNERS, CAP), 0, 1024) + 2048 * is_hot[:, None]
        unique = scores * (OWNERS * CAP) + jnp.arange(OWNERS * CAP).reshape(OWNERS, CAP)
        unused, picked = lax.top_k(unique.reshape(-1), pairs)
        owner = jax.random.permutation(order_key, picked // CAP)
        local = jax.random.randint(local_key, (pairs,), 0, ABD)
        return (owner * ABD + local).reshape(CLAT, KB)
    tiles = jax.vmap(one_tile)(jax.random.split(tile_keys, OWNERS))
    lat_tiles = NLAT // CLAT
    return tiles.reshape(NTILE, lat_tiles, CLAT, KB).transpose(1, 2, 0, 3).reshape(NLAT, NTILE, KB).astype(jnp.int32)


def set_ends(drawn, own_key, smallest, largest):
    place = [jax.random.randint(jax.random.fold_in(own_key, axis), (), 0, length) for axis, length in enumerate(drawn.shape)]
    longest = drawn.shape.index(max(drawn.shape))
    neighbour = place[:longest] + [(place[longest] + 1) % drawn.shape[longest]] + place[longest + 1:]
    return drawn.at[tuple(place)].set(smallest).at[tuple(neighbour)].set(largest)


def level_of(key, shape, shards, smallest, high):
    factor_of = 1.0
    for dim, parts in shards:
        steps = jax.random.uniform(jax.random.fold_in(jax.random.fold_in(key, 6), dim), (parts,), jnp.float32, smallest / len(shards), high / len(shards))
        factor_of = factor_of * jnp.repeat(jnp.exp(steps), shape[dim] // parts).reshape((-1,) + (1,) * (len(shape) - 1 - dim))
    return factor_of


def noise(own_key, dims, scale, most, cuts=(), dtype=jnp.bfloat16):
    level = level_of(own_key, dims, cuts, -0.22, 0.18) if cuts else 1.0
    drawn = jax.random.normal(own_key, dims, jnp.float32) * scale * level
    return jnp.minimum(jnp.maximum(drawn, -most), most).astype(dtype)


def setup_inputs(seed: int = 0) -> dict:
    keys = jax.random.split(jax.random.key(seed), 7)
    tracers = noise(keys[0], (NTR, LEV, NLAT, NLON), 1.0, 6.0, ((2, 4), (3, 8)), jnp.float32)
    velocity = jnp.clip(jax.random.uniform(keys[1], (2, LEV, NLAT, NLON), jnp.float32, -0.35, 0.35) * level_of(keys[1], (2, LEV, NLAT, NLON), ((2, 4), (3, 8)), -0.4, 0.0), -0.35, 0.35)
    mixing = jnp.clip(jnp.exp(math.log(0.075) - 2.014903 * jax.random.uniform(keys[2], (LEV, NLAT, NLON), jnp.float32) ** level_of(keys[2], (LEV, NLAT, NLON), ((1, 4), (2, 8)), -0.2, 0.2)), 0.01, 0.075)
    land_mask = set_ends((jax.random.randint(keys[3], (NLAT, NLON), 0, 4) < 3).astype(jnp.int32), jax.random.fold_in(keys[3], 1), 0, 1)
    remap_weights = jnp.clip(0.015625 * jax.random.uniform(keys[4], (NLAT, KB, NLON, CLON), jnp.float32) ** level_of(keys[4], (NLAT, KB, NLON, CLON), ((0, 4), (2, 8)), -0.2, 0.2), 0.0, 0.015625).astype(jnp.bfloat16)
    remap_dest = draw_remap_dest(jax.random.fold_in(keys[6], 71), 0)
    return {"tracers": tracers, "velocity": velocity, "mixing": mixing, "land_mask": land_mask, "remap_weights": remap_weights, "remap_dest": remap_dest}


def advect(values, east_vel, north_vel, mixing, ocean):
    row_vals = values[..., 1:-1, :]
    row_east = east_vel[..., 1:-1, :]
    row_mix = mixing[..., 1:-1, :]
    row_ocean = ocean[..., 1:-1, :]
    face_vel = 0.5 * (row_east[..., :-1] + row_east[..., 1:])
    face_mix = 0.5 * (row_mix[..., :-1] + row_mix[..., 1:])
    face_open = row_ocean[..., :-1] * row_ocean[..., 1:]
    flux_east = face_open * (jnp.maximum(face_vel, 0.0) * row_vals[..., :-1] + jnp.minimum(face_vel, 0.0) * row_vals[..., 1:] - face_mix * (row_vals[..., 1:] - row_vals[..., :-1]))
    col_vals = values[..., 1:-1]
    col_north = north_vel[..., 1:-1]
    col_mix = mixing[..., 1:-1]
    col_ocean = ocean[..., 1:-1]
    face_vnorth = 0.5 * (col_north[..., :-1, :] + col_north[..., 1:, :])
    face_mnorth = 0.5 * (col_mix[..., :-1, :] + col_mix[..., 1:, :])
    open_north = col_ocean[..., :-1, :] * col_ocean[..., 1:, :]
    flux_north = open_north * (jnp.maximum(face_vnorth, 0.0) * col_vals[..., :-1, :] + jnp.minimum(face_vnorth, 0.0) * col_vals[..., 1:, :] - face_mnorth * (col_vals[..., 1:, :] - col_vals[..., :-1, :]))
    return values[..., 1:-1, 1:-1] - (flux_east[..., 1:] - flux_east[..., :-1]) - (flux_north[..., 1:, :] - flux_north[..., :-1, :])


def extend(array):
    widths = [(0, 0)] * (array.ndim - 2) + [(1, 1), (0, 0)]
    padded = jnp.pad(array, widths)
    return jnp.concatenate([padded[..., -1:], padded, padded[..., :1]], axis=-1)


def reference(tracers, velocity, mixing, land_mask, remap_weights, remap_dest):
    ocean = land_mask.astype(jnp.float32)
    east_pad = extend(velocity[0])
    north_pad = extend(velocity[1])
    mix_pad = extend(mixing)
    ocean_pad = extend(ocean)
    values = tracers
    for step in range(STEPS):
        values = advect(extend(values), east_pad, north_pad, mix_pad, ocean_pad)
    surface = jnp.concatenate([values[:, 0] * ocean[None], ocean[None]], axis=0).astype(jnp.bfloat16)
    surface = lax.optimization_barrier(surface).astype(jnp.float32)
    rows = surface.reshape(NTR + 1, NLAT, NTILE, CLON).transpose(1, 0, 2, 3)
    weights = remap_weights.reshape(NLAT, KB, NTILE, CLON, CLON)

    def per_row(item):
        row_vals, row_weights = item
        return jnp.einsum("ftc,ktcd->tkfd", row_vals, row_weights.astype(jnp.float32), precision=lax.Precision.HIGHEST)

    partial_value = lax.map(per_row, (rows, weights))
    atmo_fields = jax.ops.segment_sum(partial_value.reshape(-1, NTR + 1, CLON), remap_dest.reshape(-1).astype(jnp.int32), num_segments=ATB)
    return values, atmo_fields
```

```python
import functools

import jax
import jax.numpy as jnp
from jax import lax
from jax.experimental import pallas as pl
from jax.experimental.pallas import tpu as pltpu
from jax.sharding import PartitionSpec as P

STEPS = 4
ABD = 16
NTR = 4
FIELDS = 8
OFF = 16
GROUP = 48
AXES = ("gx", "gy")


def lane_ids(rows):
    return lax.broadcasted_iota(jnp.int32, (rows, 128), 1)


def sub_ids(rows):
    return lax.broadcasted_iota(jnp.int32, (rows, 128), 0)


def lat_pack_kernel(has_ocean, *refs):
    if has_ocean:
        tl, vl, ml, ol, th, vh, mh, oh, south_ref, north_ref = refs
    else:
        tl, vl, ml, th, vh, mh, south_ref, north_ref = refs
        ol = oh = None
    top = sub_ids(8) < 4

    def fields(t, v, m, o):
        out = [t[i, 0] for i in range(NTR)] + [v[0, 0], v[1, 0], m[0]]
        out.append(m[0] if o is None else o[...].astype(jnp.float32))
        return out

    low, high = fields(tl, vl, ml, ol), fields(th, vh, mh, oh)
    for p in range(FIELDS // 2):
        a, b = low[2 * p], low[2 * p + 1]
        south_ref[0, 8 * p : 8 * p + 8] = jnp.where(top, a, pltpu.roll(b, 4, 0))
        a, b = high[2 * p], high[2 * p + 1]
        north_ref[0, 8 * p : 8 * p + 8] = jnp.where(top, pltpu.roll(a, 4, 0), b)


def lat_pack(tracers, velocity, mixing, ocean, first, levels):
    rows = tracers.shape[2]
    last = rows // 8 - 1
    has_ocean = ocean is not None

    def specs(block):
        out = [
            pl.BlockSpec((NTR, 1, 8, 128), lambda l: (0, l + first, block, 0)),
            pl.BlockSpec((2, 1, 8, 128), lambda l: (0, l + first, block, 0)),
            pl.BlockSpec((1, 8, 128), lambda l: (l + first, block, 0)),
        ]
        if has_ocean:
            out.append(pl.BlockSpec((8, 128), lambda l: (block, 0)))
        return out

    arrays = [tracers, velocity, mixing] + ([ocean] if has_ocean else [])
    strip = jax.ShapeDtypeStruct((levels, 32, 128), jnp.float32)
    return pl.pallas_call(
        functools.partial(lat_pack_kernel, has_ocean),
        grid=(levels,),
        in_specs=specs(0) + specs(last),
        out_specs=[pl.BlockSpec((1, 32, 128), lambda l: (l, 0, 0))] * 2,
        out_shape=[strip, strip],
        name="lat_pack",
    )(*arrays, *arrays)


def lat_halo_blocks(from_south, from_north, f):
    p, odd = f // 2, f % 2
    s = from_south[0, 8 * p : 8 * p + 8]
    n = from_north[0, 8 * p : 8 * p + 8]
    if odd:
        return s, pltpu.roll(n, 4, 0)
    return pltpu.roll(s, 4, 0), n


def interior(t, v, m, o, f):
    if f < NTR:
        return t[f, 0]
    if f < NTR + 2:
        return v[f - NTR, 0]
    if f == NTR + 2:
        return m[0]
    return o[...].astype(jnp.float32)


def lon_pack_kernel(has_ocean, *refs):
    if has_ocean:
        t, v, m, o, fs, fn, west_ref, east_ref = refs
    else:
        t, v, m, fs, fn, west_ref, east_ref = refs
        o = None
    rows = t.shape[2]
    lane = lane_ids(GROUP)
    groups = (rows + 16) // GROUP
    west = jnp.zeros((GROUP, 128), jnp.float32)
    east = jnp.zeros((GROUP, 128), jnp.float32)
    for f in range(FIELDS if has_ocean else FIELDS - 1):
        s, n = lat_halo_blocks(fs, fn, f)
        whole = jnp.concatenate([s, interior(t, v, m, o, f), n], axis=0)
        for g in range(groups):
            at = 32 * g + 4 * f
            moved = pltpu.roll(whole[GROUP * g : GROUP * g + GROUP], (at - 124) % 128, 1)
            east = jnp.where((lane >= at) & (lane < at + 4), moved, east)
            west = jnp.where((lane >= at + 4) & (lane < at + 8), moved, west)
    west_ref[0] = west
    east_ref[0] = east


def lon_pack(tracers, velocity, mixing, ocean, from_south, from_north, first, levels):
    rows = tracers.shape[2]
    has_ocean = ocean is not None
    strip = jax.ShapeDtypeStruct((levels, GROUP, 128), jnp.float32)
    specs = tile_specs(rows, lambda l: l + first, has_ocean)
    arrays = [tracers, velocity, mixing] + ([ocean] if has_ocean else [])
    return pl.pallas_call(
        functools.partial(lon_pack_kernel, has_ocean),
        grid=(levels,),
        in_specs=specs + [pl.BlockSpec((1, 32, 128), lambda l: (l, 0, 0))] * 2,
        out_specs=[pl.BlockSpec((1, GROUP, 128), lambda l: (l, 0, 0))] * 2,
        out_shape=[strip, strip],
        name="lon_pack",
    )(*arrays, from_south, from_north)


def tile_specs(rows, level, has_ocean):
    out = [
        pl.BlockSpec((NTR, 1, rows, 128), lambda l: (0, level(l), 0, 0)),
        pl.BlockSpec((2, 1, rows, 128), lambda l: (0, level(l), 0, 0)),
        pl.BlockSpec((1, rows, 128), lambda l: (level(l), 0, 0)),
    ]
    if has_ocean:
        out.append(pl.BlockSpec((rows, 128), lambda l: (0, 0)))
    return out


def unpack_field(ext, f, t, v, m, o, fs, fn, even, odd):
    rows = t.shape[2]
    s, n = lat_halo_blocks(fs, fn, f)
    ext[0, OFF - 8 : OFF] = s
    ext[0, OFF : OFF + rows] = interior(t, v, m, o, f)
    ext[0, OFF + rows : OFF + rows + 8] = n
    strip = odd if f % 2 else even
    for g in range((rows + 16) // GROUP):
        base = OFF - 8 + GROUP * g
        ext[1, base : base + GROUP] = pltpu.roll(strip, (124 - (32 * g + 4 * f)) % 128, 1)


def strips(fw, fe):
    near = lane_ids(GROUP) % 8 < 4
    w, e = fw[0], fe[0]
    return jnp.where(near, w, e), jnp.where(near, e, w)


def to_right(a, b):
    end = lane_ids(a.shape[0]) == 127
    ra, rb = pltpu.roll(a, 127, 1), pltpu.roll(b, 127, 1)
    return jnp.where(end, rb, ra), jnp.where(end, ra, rb)


def to_left(a, b):
    start = lane_ids(a.shape[0]) == 0
    ra, rb = pltpu.roll(a, 1, 1), pltpu.roll(b, 1, 1)
    return jnp.where(start, rb, ra), jnp.where(start, ra, rb)


CHUNK = 24


def chunks(rows):
    return range(OFF - 8, OFF + rows + 8, CHUNK)


def coefficients(rows, u, v, k, oc, coef, north_a, north_b):
    for r in chunks(rows):
        here, above = slice(r, r + CHUNK), slice(r + 1, r + CHUNK + 1)
        for h in range(2):
            vel = 0.5 * (v[h, here] + v[h, above])
            mix = 0.5 * (k[h, here] + k[h, above])
            face = oc[h, here] * oc[h, above]
            north_a[h, here] = face * (jnp.maximum(vel, 0.0) + mix)
            north_b[h, here] = face * (jnp.minimum(vel, 0.0) - mix)
    for r in chunks(rows):
        here, below = slice(r, r + CHUNK), slice(r - 1, r + CHUNK - 1)
        us, ks, os = ((x[0, here], x[1, here]) for x in (u, k, oc))
        ur, kr, orr = to_right(*us), to_right(*ks), to_right(*os)
        east_a, east_b = [], []
        for h in range(2):
            vel = 0.5 * (us[h] + ur[h])
            mix = 0.5 * (ks[h] + kr[h])
            face = os[h] * orr[h]
            east_a.append(face * (jnp.maximum(vel, 0.0) + mix))
            east_b.append(face * (jnp.minimum(vel, 0.0) - mix))
        west_a, west_b = to_left(*east_a), to_left(*east_b)
        for h in range(2):
            coef[0, h, here] = (
                1.0 - (east_a[h] - west_b[h]) - (north_a[h, here] - north_b[h, below])
            )
            coef[1, h, here] = -east_b[h]
            coef[2, h, here] = west_a[h]
            coef[3, h, here] = -north_b[h, here]
            coef[4, h, here] = north_a[h, below]


def advance(rows, coef, q):
    for step in range(STEPS):
        src, dst = step % 2, (step + 1) % 2
        for r in chunks(rows):
            here = slice(r, r + CHUNK)
            c = [[coef[i, h, here] for h in range(2)] for i in range(5)]
            for i in range(NTR):
                mid = [q[src, i, h, here] for h in range(2)]
                right, left = to_right(*mid), to_left(*mid)
                for h in range(2):
                    up = q[src, i, h, r + 1 : r + CHUNK + 1]
                    down = q[src, i, h, r - 1 : r + CHUNK - 1]
                    q[dst, i, h, here] = (
                        c[0][h] * mid[h]
                        + c[1][h] * right[h]
                        + c[2][h] * left[h]
                        + c[3][h] * up
                        + c[4][h] * down
                    )


def field_scratch(rows):
    ext = (2, rows + 32, 128)
    return [
        pltpu.VMEM((4,) + ext, jnp.float32),
        pltpu.VMEM((2,) + ext, jnp.float32),
        pltpu.VMEM((5,) + ext, jnp.float32),
        pltpu.VMEM((2, NTR) + ext, jnp.float32),
    ]


def run_level(rows, t, v, m, o, fs, fn, fw, fe, vel, north, coef, q):
    even, odd = strips(fw, fe)
    for i in range(NTR):
        unpack_field(q.at[0, i], i, t, v, m, o, fs, fn, even, odd)
    for i in range(3):
        unpack_field(vel.at[i], NTR + i, t, v, m, o, fs, fn, even, odd)
    coefficients(
        rows, vel.at[0], vel.at[1], vel.at[2], vel.at[3], coef, north.at[0], north.at[1]
    )
    advance(rows, coef, q)


def surface_kernel(
    order, accs, slot, t, v, m, o, fs, fn, fw, fe, w, out_q, out_send, out_keep,
    vel, north, coef, q, surf, *sums,
):
    rows = t.shape[2]
    even, odd = strips(fw, fe)
    unpack_field(vel.at[3], FIELDS - 1, t, v, m, o, fs, fn, even, odd)
    run_level(rows, t, v, m, o, fs, fn, fw, fe, vel, north, coef, q)
    ocean = o[...].astype(jnp.float32)
    for i in range(NTR):
        done = q[0, i, 0, OFF : OFF + rows]
        out_q[i] = done
        surf[pl.ds(i, rows, stride=8), :] = done * ocean
    surf[pl.ds(NTR, rows, stride=8), :] = ocean
    for i in range(NTR + 1, 8):
        surf[pl.ds(i, rows, stride=8), :] = jnp.zeros((rows, 128), jnp.float32)
    for d in sums:
        d[...] = jnp.zeros_like(d)
    first = sub_ids(16) < 8
    kb = w.shape[1]

    def body(i, carry):
        s = surf[pl.ds(pl.multiple_of(16 * i, 16), 16), :]
        lhs = jnp.concatenate(
            [jnp.where(first, s, 0.0), jnp.where(first, 0.0, s)], axis=1
        ).astype(jnp.bfloat16)
        for k in range(0, kb, 2):
            rhs = jnp.concatenate(
                [
                    jnp.concatenate([w[2 * i + r, k], w[2 * i + r, k + 1]], axis=1)
                    for r in range(2)
                ],
                axis=0,
            )
            part = jnp.dot(lhs, rhs, preferred_element_type=jnp.float32)
            for r in range(2):
                for kk in range(2):
                    d = sums[(k + kk) % accs]
                    at = pl.ds(
                        pl.multiple_of(8 * slot[(2 * i + r) * kb + k + kk], 8), 8
                    )
                    d[at, :] += part[8 * r : 8 * r + 8, 128 * kk : 128 * kk + 128]
        return carry

    lax.fori_loop(0, rows // 2, body, 0, unroll=2)
    chunk = ABD * (NTR + 1)
    half = len(order) // 2
    for place, owner in enumerate(order):
        ref, base = (out_keep, place) if place < half else (out_send, place - half)
        for f in range(NTR + 1):
            total = sums[0][pl.ds(owner * ABD * 8 + f, ABD, stride=8), :]
            for d in sums[1:]:
                total = total + d[pl.ds(owner * ABD * 8 + f, ABD, stride=8), :]
            at = base * chunk + f * ABD
            ref[at : at + ABD, :] = total


def surface(order, slot, tracers, velocity, mixing, ocean, halo, weights):
    rows = tracers.shape[2]
    owners = len(order)
    accs = 4 if owners <= 32 else 1
    strip = [pl.BlockSpec((1, 32, 128), lambda l, s: (0, 0, 0))] * 2
    strip += [pl.BlockSpec((1, GROUP, 128), lambda l, s: (0, 0, 0))] * 2
    tiles = [
        pl.BlockSpec((NTR, 1, rows, 128), lambda l, s: (0, 0, 0, 0)),
        pl.BlockSpec((2, 1, rows, 128), lambda l, s: (0, 0, 0, 0)),
        pl.BlockSpec((1, rows, 128), lambda l, s: (0, 0, 0)),
        pl.BlockSpec((rows, 128), lambda l, s: (0, 0)),
    ]
    half = owners // 2 * ABD * (NTR + 1)
    return pl.pallas_call(
        functools.partial(surface_kernel, order, accs),
        grid_spec=pltpu.PrefetchScalarGridSpec(
            num_scalar_prefetch=1,
            grid=(1,),
            in_specs=tiles + strip + [pl.BlockSpec(memory_space=pltpu.VMEM)],
            out_specs=[
                pl.BlockSpec((NTR, rows, 128), lambda l, s: (0, 0, 0)),
                pl.BlockSpec(memory_space=pltpu.VMEM),
                pl.BlockSpec(memory_space=pltpu.VMEM),
            ],
            scratch_shapes=field_scratch(rows)
            + [pltpu.VMEM((rows * 8, 128), jnp.float32)]
            + [pltpu.VMEM((owners * ABD * 8, 128), jnp.float32)] * accs,
        ),
        out_shape=[
            jax.ShapeDtypeStruct((NTR, rows, 128), jnp.float32),
            jax.ShapeDtypeStruct((half, 128), jnp.float32),
            jax.ShapeDtypeStruct((half, 128), jnp.float32),
        ],
        compiler_params=pltpu.CompilerParams(vmem_limit_bytes=48 << 20),
        name="surface",
    )(slot, tracers, velocity, mixing, ocean, *halo, weights)


def deep_kernel(t, v, m, o, fs, fn, fw, fe, ofs, ofn, ofw, ofe, done, out, vel, north, coef, q):
    rows = t.shape[2]
    level = pl.program_id(0)

    @pl.when(level == 0)
    def _():
        out[:, 0] = done[...]
        even, odd = strips(ofw, ofe)
        unpack_field(vel.at[3], FIELDS - 1, t, v, m, o, ofs, ofn, even, odd)

    @pl.when(level > 0)
    def _():
        run_level(rows, t, v, m, o, fs, fn, fw, fe, vel, north, coef, q)
        for i in range(NTR):
            out[i, 0] = q[0, i, 0, OFF : OFF + rows]


def deep(tracers, velocity, mixing, ocean, halo, ocean_halo, done):
    rows, levels = tracers.shape[2], tracers.shape[1]
    specs = tile_specs(rows, lambda l: jnp.maximum(l, 1), True)
    strip = [pl.BlockSpec((1, 32, 128), lambda l: (jnp.maximum(l - 1, 0), 0, 0))] * 2
    strip += [pl.BlockSpec((1, GROUP, 128), lambda l: (jnp.maximum(l - 1, 0), 0, 0))] * 2
    fixed = [pl.BlockSpec((1, 32, 128), lambda l: (0, 0, 0))] * 2
    fixed += [pl.BlockSpec((1, GROUP, 128), lambda l: (0, 0, 0))] * 2
    return pl.pallas_call(
        deep_kernel,
        grid=(levels,),
        in_specs=specs + strip + fixed
        + [pl.BlockSpec((NTR, rows, 128), lambda l: (0, 0, 0))],
        out_specs=pl.BlockSpec((NTR, 1, rows, 128), lambda l: (0, l, 0, 0)),
        out_shape=jax.ShapeDtypeStruct(tracers.shape, jnp.float32),
        scratch_shapes=field_scratch(rows),
        compiler_params=pltpu.CompilerParams(vmem_limit_bytes=24 << 20),
        name="deep",
    )(tracers, velocity, mixing, ocean, *halo, *ocean_halo, done)


def exchange_lat(to_south, to_north):
    n = lax.axis_size("gy")
    from_south = lax.ppermute(to_north, "gy", [(i, i + 1) for i in range(n - 1)])
    from_north = lax.ppermute(to_south, "gy", [(i + 1, i) for i in range(n - 1)])
    return from_south, from_north


def exchange_lon(to_west, to_east):
    n = lax.axis_size("gx")
    from_west = lax.ppermute(to_east, "gx", [(i, (i + 1) % n) for i in range(n)])
    from_east = lax.ppermute(to_west, "gx", [((i + 1) % n, i) for i in range(n)])
    return from_west, from_east


def partner(a, mask, n):
    return lax.ppermute(a, AXES, [(i, i ^ mask) for i in range(n)])


def rounds_of(owners):
    bits = owners.bit_length() - 1
    out, at = [(0, 1)], 1
    while at < bits:
        width = min(2, bits - at)
        out.append((at, width))
        at += width
    return out


def order_of(owners):
    def key(owner):
        return tuple((owner >> at) & ((1 << width) - 1) for at, width in rounds_of(owners))
    return sorted(range(owners), key=key)


def per_device(tracers, velocity, mixing, land_mask, remap_weights, remap_dest):
    owners = lax.axis_size("gx") * lax.axis_size("gy")
    levels = tracers.shape[1]
    me = lax.axis_index("gx") * lax.axis_size("gy") + lax.axis_index("gy")
    dest = remap_dest.reshape(-1)
    slot = jnp.bitwise_xor(dest // ABD, me) * ABD + dest % ABD

    lat0 = exchange_lat(*lat_pack(tracers, velocity, mixing, land_mask, 0, 1))
    lon0 = exchange_lon(*lon_pack(tracers, velocity, mixing, land_mask, *lat0, 0, 1))
    halo0 = lat0 + lon0
    lat1 = exchange_lat(*lat_pack(tracers, velocity, mixing, None, 1, levels - 1))
    lon1 = exchange_lon(*lon_pack(tracers, velocity, mixing, None, *lat1, 1, levels - 1))
    halo1 = lat1 + lon1

    order = order_of(owners)
    done, send, keep = surface(
        order, slot, tracers, velocity, mixing, land_mask, halo0, remap_weights
    )
    values = deep(tracers, velocity, mixing, land_mask, halo1, halo0, done)

    total = keep + partner(send, 1, owners)
    for at, width in rounds_of(owners)[1:]:
        parts = total.reshape((1 << width, -1, 128))
        got = [partner(parts[i], i << at, owners) for i in range(1, 1 << width)]
        total = parts[0]
        for g in got:
            total = total + g
    atmo = total.reshape(NTR + 1, ABD, 128).transpose(1, 0, 2)
    return values, atmo


def solution(mesh):
    placed = (
        P(None, None, "gy", "gx"),
        P(None, None, "gy", "gx"),
        P(None, "gy", "gx"),
        P("gy", "gx"),
        P("gy", None, "gx", None),
        P("gy", "gx", None),
    )
    return jax.shard_map(
        per_device,
        mesh=mesh,
        in_specs=placed,
        out_specs=(P(None, None, "gy", "gx"), P(("gx", "gy"), None, None)),
        check_vma=False,
    )
```

```python
import functools

import jax
import jax.numpy as jnp
from jax import lax
from jax.experimental import pallas as pl
from jax.experimental.pallas import tpu as pltpu
from jax.sharding import PartitionSpec as P

STEPS = 4
ABD = 16
NTR = 4
FIELDS = 8
OFF = 16
FETCHES = 1
GROUP = 48
AXES = ("gx", "gy")


WHOLE = pl.BlockSpec(memory_space=pltpu.VMEM)


def took(us):
    return pl.CostEstimate(flops=0, bytes_accessed=int(us * 3.5e6), transcendentals=0)


def lane_ids(rows):
    return lax.broadcasted_iota(jnp.int32, (rows, 128), 1)


def sub_ids(rows):
    return lax.broadcasted_iota(jnp.int32, (rows, 128), 0)


def lat_pack_kernel(tl, vl, ml, ol, th, vh, mh, oh, south_ref, north_ref):
    top = sub_ids(8) < 4
    for level in range(tl.shape[1]):

        def fields(t, v, m, o):
            out = [t[i, level] for i in range(NTR)] + [v[0, level], v[1, level], m[level]]
            out.append(o[...].astype(jnp.float32) if level == 0 else m[level])
            return out

        low, high = fields(tl, vl, ml, ol), fields(th, vh, mh, oh)
        for p in range(FIELDS // 2):
            a, b = low[2 * p], low[2 * p + 1]
            south_ref[level, 8 * p : 8 * p + 8] = jnp.where(top, a, pltpu.roll(b, 4, 0))
            a, b = high[2 * p], high[2 * p + 1]
            north_ref[level, 8 * p : 8 * p + 8] = jnp.where(top, pltpu.roll(a, 4, 0), b)


def lat_pack(tracers, velocity, mixing, ocean):
    levels, rows = tracers.shape[1:3]
    last = rows // 8 - 1

    def specs(block):
        return [
            pl.BlockSpec((NTR, levels, 8, 128), lambda l: (0, 0, block, 0)),
            pl.BlockSpec((2, levels, 8, 128), lambda l: (0, 0, block, 0)),
            pl.BlockSpec((levels, 8, 128), lambda l: (0, block, 0)),
            pl.BlockSpec((8, 128), lambda l: (block, 0)),
        ]

    arrays = [tracers, velocity, mixing, ocean]
    strip = jax.ShapeDtypeStruct((levels, 32, 128), jnp.float32)
    return pl.pallas_call(
        lat_pack_kernel,
        grid=(1,),
        in_specs=specs(0) + specs(last),
        out_specs=[WHOLE] * 2,
        out_shape=[strip, strip],
        cost_estimate=took(2),
        name="lat_pack",
    )(*arrays, *arrays)


def lat_halo_blocks(from_south, from_north, f, level):
    p, odd = f // 2, f % 2
    s = from_south[level, 8 * p : 8 * p + 8]
    n = from_north[level, 8 * p : 8 * p + 8]
    if odd:
        return s, pltpu.roll(n, 4, 0)
    return pltpu.roll(s, 4, 0), n


def interior(t, v, m, o, f, level):
    if f < NTR:
        return t[f, level]
    if f < NTR + 2:
        return v[f - NTR, level]
    if f == NTR + 2:
        return m[level]
    return o[...].astype(jnp.float32)


def fetch(part, parts, w, out, sem):
    rows = w.shape[0] // parts
    return pltpu.make_async_copy(w.at[pl.ds(part * rows, rows)], out, sem)


def fetched(w, parts):
    return pltpu.VMEM((w.shape[0] // parts,) + w.shape[1:], w.dtype)


def lon_pack_kernel(first, fetching, t, v, m, o, fs, fn, *refs):
    if fetching is None:
        lon_pack_body(first, t, v, m, o, fs, fn, *refs)
        return
    w, west_ref, east_ref, out, sem = refs
    copy = fetch(*fetching, w, out, sem)
    copy.start()
    lon_pack_body(first, t, v, m, o, fs, fn, west_ref, east_ref)
    copy.wait()


def lon_pack_body(first, t, v, m, o, fs, fn, west_ref, east_ref):
    rows = t.shape[2]
    lane = lane_ids(GROUP)
    groups = (rows + 16) // GROUP
    for l in range(west_ref.shape[0]):
        level = first + l
        west = jnp.zeros((GROUP, 128), jnp.float32)
        east = jnp.zeros((GROUP, 128), jnp.float32)
        for f in range(FIELDS if level == 0 else FIELDS - 1):
            s, n = lat_halo_blocks(fs, fn, f, level)
            whole = jnp.concatenate([s, interior(t, v, m, o, f, level), n], axis=0)
            for g in range(groups):
                at = 32 * g + 4 * f
                moved = pltpu.roll(whole[GROUP * g : GROUP * g + GROUP], (at - 124) % 128, 1)
                east = jnp.where((lane >= at) & (lane < at + 4), moved, east)
                west = jnp.where((lane >= at + 4) & (lane < at + 8), moved, west)
        west_ref[l] = west
        east_ref[l] = east


def lon_pack(tracers, velocity, mixing, ocean, from_south, from_north, first, levels,
             fetching=None, weights=None):
    strip = jax.ShapeDtypeStruct((levels, GROUP, 128), jnp.float32)
    more = [] if fetching is None else [pl.BlockSpec(memory_space=pltpu.HBM)]
    out = [] if fetching is None else [fetched(weights, fetching[1])]
    return pl.pallas_call(
        functools.partial(lon_pack_kernel, first, fetching),
        in_specs=[WHOLE] * 6 + more,
        out_specs=[WHOLE] * (2 + len(out)),
        out_shape=[strip, strip] + out,
        scratch_shapes=[pltpu.SemaphoreType.DMA] * len(out),
        compiler_params=pltpu.CompilerParams(vmem_limit_bytes=4 << 20),
        cost_estimate=took(0.6 * levels),
        name="lon_pack",
    )(tracers, velocity, mixing, ocean, from_south, from_north, *([weights] if more else []))


def unpack_field(ext, f, level, t, v, m, o, fs, fn, even, odd):
    rows = t.shape[2]
    s, n = lat_halo_blocks(fs, fn, f, level)
    ext[0, OFF - 8 : OFF] = s
    ext[0, OFF : OFF + rows] = interior(t, v, m, o, f, level)
    ext[0, OFF + rows : OFF + rows + 8] = n
    strip = odd if f % 2 else even
    for g in range((rows + 16) // GROUP):
        base = OFF - 8 + GROUP * g
        ext[1, base : base + GROUP] = pltpu.roll(strip, (124 - (32 * g + 4 * f)) % 128, 1)


def strips(fw, fe, l):
    near = lane_ids(GROUP) % 8 < 4
    w, e = fw[l], fe[l]
    return jnp.where(near, w, e), jnp.where(near, e, w)


def to_right(a, b):
    end = lane_ids(a.shape[0]) == 127
    ra, rb = pltpu.roll(a, 127, 1), pltpu.roll(b, 127, 1)
    return jnp.where(end, rb, ra), jnp.where(end, ra, rb)


def to_left(a, b):
    start = lane_ids(a.shape[0]) == 0
    ra, rb = pltpu.roll(a, 1, 1), pltpu.roll(b, 1, 1)
    return jnp.where(start, rb, ra), jnp.where(start, ra, rb)


CHUNK = 24


def chunks(rows):
    return range(OFF - 8, OFF + rows + 8, CHUNK)


def faces(a, b, mix, face):
    vel = a + b
    low = jnp.maximum(vel, 0.0) + mix
    return face * low, face * (low - vel)


def coefficients(rows, u, v, k, oc, coef, north):
    for r in chunks(rows):
        here, above = slice(r, r + CHUNK), slice(r + 1, r + CHUNK + 1)
        for h in range(2):
            face = 0.5 * (oc[h, here] * oc[h, above])
            na, nb = faces(v[h, here], v[h, above], k[h, here] + k[h, above], face)
            north[h, here] = na
            coef[3, h, here] = nb
    for r in chunks(rows):
        here, below = slice(r, r + CHUNK), slice(r - 1, r + CHUNK - 1)
        us, ks, os = ((x[0, here], x[1, here]) for x in (u, k, oc))
        ur, kr, orr = to_right(*us), to_right(*ks), to_right(*os)
        ea, eb = [], []
        for h in range(2):
            a, b = faces(us[h], ur[h], ks[h] + kr[h], 0.5 * (os[h] * orr[h]))
            ea.append(a)
            eb.append(b)
        wa, wb = to_left(*ea), to_left(*eb)
        for h in range(2):
            south = north[h, below]
            coef[0, h, here] = (1.0 - (ea[h] + wb[h])) - (north[h, here] + coef[3, h, below])
            coef[1, h, here] = eb[h]
            coef[2, h, here] = wa[h]
            coef[4, h, here] = south


def advance(rows, coef, q):
    for step in range(STEPS):
        src, dst = step % 2, (step + 1) % 2
        for r in chunks(rows):
            here = slice(r, r + CHUNK)
            c = [[coef[i, h, here] for h in range(2)] for i in range(5)]
            for i in range(NTR):
                mid = [q[src, i, h, here] for h in range(2)]
                right, left = to_right(*mid), to_left(*mid)
                for h in range(2):
                    up = q[src, i, h, r + 1 : r + CHUNK + 1]
                    down = q[src, i, h, r - 1 : r + CHUNK - 1]
                    q[dst, i, h, here] = (
                        c[0][h] * mid[h]
                        + c[1][h] * right[h]
                        + c[2][h] * left[h]
                        + c[3][h] * up
                        + c[4][h] * down
                    )


def field_scratch(rows):
    ext = (2, rows + 32, 128)
    return [
        pltpu.VMEM((4,) + ext, jnp.float32),
        pltpu.VMEM(ext, jnp.float32),
        pltpu.VMEM((5,) + ext, jnp.float32),
        pltpu.VMEM((2, NTR) + ext, jnp.float32),
    ]


def run_level(rows, level, l, t, v, m, o, fs, fn, fw, fe, vel, north, coef, q):
    even, odd = strips(fw, fe, l)
    for i in range(NTR):
        unpack_field(q.at[0, i], i, level, t, v, m, o, fs, fn, even, odd)
    for i in range(3):
        unpack_field(vel.at[i], NTR + i, level, t, v, m, o, fs, fn, even, odd)
    coefficients(rows, vel.at[0], vel.at[1], vel.at[2], vel.at[3], coef, north)
    advance(rows, coef, q)


def unpack_ocean(t, v, m, o, fs, fn, fw, fe, vel):
    even, odd = strips(fw, fe, 0)
    unpack_field(vel.at[3], FIELDS - 1, 0, t, v, m, o, fs, fn, even, odd)


def surface_kernel(
    order, accs, slot, t, v, m, o, fs, fn, fw, fe, *refs):
    surface_body(order, accs, slot, t, v, m, o, fs, fn, fw, fe, refs[:FETCHES], *refs[FETCHES:])


def surface_body(
    order, accs, slot, t, v, m, o, fs, fn, fw, fe, ws, out_q, out_send, out_keep,
    vel, north, coef, q, surf, *sums,
):
    rows = t.shape[2]
    unpack_ocean(t, v, m, o, fs, fn, fw, fe, vel)
    run_level(rows, 0, 0, t, v, m, o, fs, fn, fw, fe, vel, north, coef, q)
    ocean = o[...].astype(jnp.float32)
    for i in range(NTR):
        done = q[0, i, 0, OFF : OFF + rows]
        out_q[i] = done
        surf[pl.ds(i, rows, stride=8), :] = done * ocean
    surf[pl.ds(NTR, rows, stride=8), :] = ocean
    for i in range(NTR + 1, 8):
        surf[pl.ds(i, rows, stride=8), :] = jnp.zeros((rows, 128), jnp.float32)
    for d in sums:
        d[...] = jnp.zeros_like(d)
    first = sub_ids(16) < 8
    kb = ws[0].shape[1]
    per = rows // FETCHES // 2

    def body(w, base, i, carry):
        j = i + base
        s = surf[pl.ds(pl.multiple_of(16 * j, 16), 16), :]
        lhs = jnp.concatenate(
            [jnp.where(first, s, 0.0), jnp.where(first, 0.0, s)], axis=1
        ).astype(jnp.bfloat16)
        for k in range(0, kb, 2):
            rhs = jnp.concatenate(
                [
                    jnp.concatenate([w[2 * i + r, k], w[2 * i + r, k + 1]], axis=1)
                    for r in range(2)
                ],
                axis=0,
            )
            part = jnp.dot(lhs, rhs, preferred_element_type=jnp.float32)
            for r in range(2):
                for kk in range(2):
                    d = sums[(k + kk) % accs]
                    at = pl.ds(
                        pl.multiple_of(8 * slot[(2 * j + r) * kb + k + kk], 8), 8
                    )
                    d[at, :] += part[8 * r : 8 * r + 8, 128 * kk : 128 * kk + 128]
        return carry

    for n, w in enumerate(ws):
        lax.fori_loop(0, per, functools.partial(body, w, n * per), 0, unroll=16)
    chunk = ABD * (NTR + 1)
    half = len(order) // 2
    for place, owner in enumerate(order):
        ref, base = (out_keep, place) if place < half else (out_send, place - half)
        for f in range(NTR + 1):
            total = sums[0][pl.ds(owner * ABD * 8 + f, ABD, stride=8), :]
            for d in sums[1:]:
                total = total + d[pl.ds(owner * ABD * 8 + f, ABD, stride=8), :]
            at = base * chunk + f * ABD
            ref[at : at + ABD, :] = total


def surface(order, slot, tracers, velocity, mixing, ocean, halo, weights):
    rows = tracers.shape[2]
    owners = len(order)
    accs = 4 if owners <= 32 else 1
    half = owners // 2 * ABD * (NTR + 1)
    return pl.pallas_call(
        functools.partial(surface_kernel, order, accs),
        in_specs=[pl.BlockSpec(memory_space=pltpu.SMEM)] + [WHOLE] * (8 + FETCHES),
        out_specs=[WHOLE] * 3,
        scratch_shapes=field_scratch(rows)
        + [pltpu.VMEM((rows * 8, 128), jnp.float32)]
        + [pltpu.VMEM((owners * ABD * 8, 128), jnp.float32)] * accs,
        out_shape=[
            jax.ShapeDtypeStruct((NTR, rows, 128), jnp.float32),
            jax.ShapeDtypeStruct((half, 128), jnp.float32),
            jax.ShapeDtypeStruct((half, 128), jnp.float32),
        ],
        compiler_params=pltpu.CompilerParams(vmem_limit_bytes=22 << 20),
        cost_estimate=took(7),
        name="surface",
    )(slot, tracers, velocity, mixing, ocean, *halo, *weights)


def deep_kernel(first, t, v, m, o, fs, fn, fw, fe, ofw, ofe, base, out, vel, north, coef, q):
    rows = t.shape[2]
    level = pl.program_id(0) + first

    @pl.when(pl.program_id(0) == 0)
    def _():
        unpack_ocean(t, v, m, o, fs, fn, ofw, ofe, vel)

    if first == 0:
        @pl.when(level == 0)
        def _():
            out[:, 0] = base[...]

    @pl.when(level > 0)
    def _():
        run_level(rows, level, level - 1, t, v, m, o, fs, fn, fw, fe, vel, north, coef, q)
        for i in range(NTR):
            out[i, 0] = q[0, i, 0, OFF : OFF + rows]


def deep(tracers, velocity, mixing, ocean, halo, ocean_halo, base, first, levels):
    rows = tracers.shape[2]
    return pl.pallas_call(
        functools.partial(deep_kernel, first),
        grid=(levels,),
        in_specs=[WHOLE] * 10 + [pl.BlockSpec(memory_space=pl.ANY) if first else WHOLE],
        out_specs=pl.BlockSpec((NTR, 1, rows, 128), lambda l: (0, l + first, 0, 0)),
        out_shape=jax.ShapeDtypeStruct(tracers.shape, jnp.float32),
        scratch_shapes=field_scratch(rows),
        input_output_aliases={10: 0} if first else {},
        compiler_params=pltpu.CompilerParams(vmem_limit_bytes=16 << 20),
        cost_estimate=took(1.8 * levels),
        name="deep",
    )(tracers, velocity, mixing, ocean, *halo, *ocean_halo, base)


def exchange_lat(to_south, to_north):
    n = lax.axis_size("gy")
    from_south = lax.ppermute(to_north, "gy", [(i, i + 1) for i in range(n - 1)])
    from_north = lax.ppermute(to_south, "gy", [(i + 1, i) for i in range(n - 1)])
    return from_south, from_north


def exchange_lon(to_west, to_east):
    n = lax.axis_size("gx")
    from_west = lax.ppermute(to_east, "gx", [(i, (i + 1) % n) for i in range(n)])
    from_east = lax.ppermute(to_west, "gx", [((i + 1) % n, i) for i in range(n)])
    return from_west, from_east


def partner(a, mask, n):
    return lax.ppermute(a, AXES, [(i, i ^ mask) for i in range(n)])


def rounds_of(owners):
    bits = owners.bit_length() - 1
    out, at = [(0, 1)], 1
    while at < bits:
        width = min(2, bits - at)
        out.append((at, width))
        at += width
    return out


def order_of(owners):
    def key(owner):
        return tuple((owner >> at) & ((1 << width) - 1) for at, width in rounds_of(owners))
    return sorted(range(owners), key=key)


def per_device(tracers, velocity, mixing, land_mask, remap_weights, remap_dest):
    remap_weights = pltpu.with_memory_space_constraint(remap_weights, pltpu.HBM)
    owners = lax.axis_size("gx") * lax.axis_size("gy")
    levels = tracers.shape[1]
    me = lax.axis_index("gx") * lax.axis_size("gy") + lax.axis_index("gy")
    dest = remap_dest.reshape(-1)
    slot = jnp.bitwise_xor(dest // ABD, me) * ABD + dest % ABD

    tile = (tracers, velocity, mixing, land_mask)
    lat = exchange_lat(*lat_pack(*tile))
    to_west, to_east = lon_pack(*tile, *lat, 0, 1)
    lon0 = exchange_lon(to_west, to_east)
    lat, to_west = lax.optimization_barrier((lat, to_west))
    packed = lon_pack(*tile, *lat, 1, levels - 1, (0, FETCHES), remap_weights)
    lon0, packed = lax.optimization_barrier((lon0, packed))
    lon1 = exchange_lon(*packed[:2])

    order = order_of(owners)
    done, send, keep = surface(order, slot, *tile, lat + lon0,
        [pltpu.with_memory_space_constraint(w, pltpu.VMEM) for w in packed[2:]],
    )
    got = partner(send, 1, owners)
    total = keep + got
    lat, total = lax.optimization_barrier((lat, total))
    values = done
    rounds = rounds_of(owners)[1:]
    cut = [0] + [levels * (i + 1) // len(rounds) for i in range(len(rounds))]
    cut[1:-1] = [c + 1 for c in cut[1:-1]]
    for i, (at, width) in enumerate(rounds):
        parts = total.reshape((1 << width, -1, 128))
        got = [partner(parts[j], j << at, owners) for j in range(1, 1 << width)]
        values = deep(*tile, lat + lon1, lon0, values, cut[i], cut[i + 1] - cut[i])
        got, values = lax.optimization_barrier((got, values))
        total = parts[0]
        for g in got:
            total = total + g
    atmo = total.reshape(NTR + 1, ABD, 128).transpose(1, 0, 2)
    return values, atmo


def solution(mesh):
    placed = (
        P(None, None, "gy", "gx"),
        P(None, None, "gy", "gx"),
        P(None, "gy", "gx"),
        P("gy", "gx"),
        P("gy", None, "gx", None),
        P("gy", "gx", None),
    )
    return jax.shard_map(
        per_device,
        mesh=mesh,
        in_specs=placed,
        out_specs=(P(None, None, "gy", "gx"), P(("gx", "gy"), None, None)),
        check_vma=False,
    )
```

```python
import functools

import jax
import jax.numpy as jnp
from jax import lax
from jax.experimental import pallas as pl
from jax.experimental.pallas import tpu as pltpu
from jax.sharding import PartitionSpec as P

STEPS = 4
ABD = 16
NTR = 4
FIELDS = 8
OFF = 16
GROUP = 48
AXES = ("gx", "gy")


WHOLE = pl.BlockSpec(memory_space=pltpu.VMEM)


def took(us):
    return pl.CostEstimate(flops=0, bytes_accessed=int(us * 3.5e6), transcendentals=0)


def in_hbm(a):
    return pltpu.with_memory_space_constraint(a, pltpu.HBM)


def lane_ids(rows):
    return lax.broadcasted_iota(jnp.int32, (rows, 128), 1)


def sub_ids(rows):
    return lax.broadcasted_iota(jnp.int32, (rows, 128), 0)


def lat_pack_kernel(tl, vl, ml, ol, th, vh, mh, oh, south_ref, north_ref):
    top = sub_ids(8) < 4
    for level in range(tl.shape[1]):

        def fields(t, v, m, o):
            out = [t[i, level] for i in range(NTR)] + [v[0, level], v[1, level], m[level]]
            out.append(o[...].astype(jnp.float32) if level == 0 else m[level])
            return out

        low, high = fields(tl, vl, ml, ol), fields(th, vh, mh, oh)
        for p in range(FIELDS // 2):
            a, b = low[2 * p], low[2 * p + 1]
            south_ref[level, 8 * p : 8 * p + 8] = jnp.where(top, a, pltpu.roll(b, 4, 0))
            a, b = high[2 * p], high[2 * p + 1]
            north_ref[level, 8 * p : 8 * p + 8] = jnp.where(top, pltpu.roll(a, 4, 0), b)


def lat_pack(tracers, velocity, mixing, ocean):
    levels, rows = tracers.shape[1:3]
    last = rows // 8 - 1

    def specs(block):
        return [
            pl.BlockSpec((NTR, levels, 8, 128), lambda l: (0, 0, block, 0)),
            pl.BlockSpec((2, levels, 8, 128), lambda l: (0, 0, block, 0)),
            pl.BlockSpec((levels, 8, 128), lambda l: (0, block, 0)),
            pl.BlockSpec((8, 128), lambda l: (block, 0)),
        ]

    arrays = [in_hbm(a) for a in (tracers, velocity, mixing, ocean)]
    strip = jax.ShapeDtypeStruct((levels, 32, 128), jnp.float32)
    return pl.pallas_call(
        lat_pack_kernel,
        grid=(1,),
        in_specs=specs(0) + specs(last),
        out_specs=[WHOLE] * 2,
        out_shape=[strip, strip],
        compiler_params=pltpu.CompilerParams(vmem_limit_bytes=4 << 20),
        cost_estimate=took(2),
        name="lat_pack",
    )(*arrays, *arrays)


def lat_halo_blocks(from_south, from_north, f, level):
    p, odd = f // 2, f % 2
    s = from_south[level, 8 * p : 8 * p + 8]
    n = from_north[level, 8 * p : 8 * p + 8]
    if odd:
        return s, pltpu.roll(n, 4, 0)
    return pltpu.roll(s, 4, 0), n


def interior(t, v, m, o, f, level):
    if f < NTR:
        return t[f, level]
    if f < NTR + 2:
        return v[f - NTR, level]
    if f == NTR + 2:
        return m[level]
    return o[...].astype(jnp.float32)


def fetch_kernel(after, w, out, sem):
    copy = pltpu.make_async_copy(w, out, sem)
    copy.start()
    copy.wait()


def fetch(weights, after):
    return pl.pallas_call(
        fetch_kernel,
        in_specs=[pl.BlockSpec(memory_space=pl.ANY), pl.BlockSpec(memory_space=pltpu.HBM)],
        out_specs=WHOLE,
        out_shape=pltpu.VMEM(weights.shape, weights.dtype),
        scratch_shapes=[pltpu.SemaphoreType.DMA],
        compiler_params=pltpu.CompilerParams(vmem_limit_bytes=2 << 20),
        cost_estimate=took(5),
        name="fetch",
    )(after, pltpu.with_memory_space_constraint(weights, pltpu.HBM))


def lon_pack_kernel(t, v, m, o_hbm, fs, fn, west_ref, east_ref, o, sem):
    copy = pltpu.make_async_copy(o_hbm, o, sem)
    copy.start()
    rows = t.shape[2]
    lane = lane_ids(GROUP)
    groups = (rows + 16) // GROUP
    levels = t.shape[1]
    for level in [*range(1, levels), 0]:
        if level == 0:
            copy.wait()
        west = east = jnp.zeros((GROUP, 128), jnp.float32)
        for f in range(FIELDS if level == 0 else FIELDS - 1):
            s, n = lat_halo_blocks(fs, fn, f, level)
            whole = jnp.concatenate([s, interior(t, v, m, o, f, level), n], axis=0)
            for g in range(groups):
                at = 32 * g + 4 * f
                part = whole[GROUP * g : GROUP * g + GROUP]
                moved = pltpu.roll(part, (at - 124) % 128, 1)
                east = jnp.where((lane >= at) & (lane < at + 4), moved, east)
                west = jnp.where((lane >= at + 4) & (lane < at + 8), moved, west)
        west_ref[level] = west
        east_ref[level] = east


def lon_pack(tracers, velocity, mixing, ocean, from_south, from_north):
    strip = jax.ShapeDtypeStruct((tracers.shape[1], GROUP, 128), jnp.float32)
    return pl.pallas_call(
        lon_pack_kernel,
        in_specs=[WHOLE] * 3 + [pl.BlockSpec(memory_space=pltpu.HBM)] + [WHOLE] * 2,
        out_specs=[WHOLE] * 2,
        out_shape=[strip, strip],
        scratch_shapes=[pltpu.VMEM(ocean.shape, ocean.dtype), pltpu.SemaphoreType.DMA],
        compiler_params=pltpu.CompilerParams(vmem_limit_bytes=4 << 20),
        cost_estimate=took(1.2),
        name="lon_pack",
    )(tracers, velocity, mixing, in_hbm(ocean), from_south, from_north)


def unpack_field(ext, f, level, t, v, m, o, fs, fn, even, odd):
    rows = t.shape[2]
    s, n = lat_halo_blocks(fs, fn, f, level)
    ext[0, OFF - 8 : OFF] = s
    ext[0, OFF : OFF + rows] = interior(t, v, m, o, f, level)
    ext[0, OFF + rows : OFF + rows + 8] = n
    strip = odd if f % 2 else even
    for g in range((rows + 16) // GROUP):
        base = OFF - 8 + GROUP * g
        ext[1, base : base + GROUP] = pltpu.roll(strip, (124 - (32 * g + 4 * f)) % 128, 1)


def strips(fw, fe, l):
    near = lane_ids(GROUP) % 8 < 4
    w, e = fw[l], fe[l]
    return jnp.where(near, w, e), jnp.where(near, e, w)


def to_right(a, b):
    end = lane_ids(a.shape[0]) == 127
    ra, rb = pltpu.roll(a, 127, 1), pltpu.roll(b, 127, 1)
    return jnp.where(end, rb, ra), jnp.where(end, ra, rb)


def to_left(a, b):
    start = lane_ids(a.shape[0]) == 0
    ra, rb = pltpu.roll(a, 1, 1), pltpu.roll(b, 1, 1)
    return jnp.where(start, rb, ra), jnp.where(start, ra, rb)


CHUNK = 24


def chunks(rows):
    return range(OFF - 8, OFF + rows + 8, CHUNK)


def faces(a, b, mix, face):
    vel = a + b
    low = jnp.maximum(vel, 0.0) + mix
    return face * low, face * (low - vel)


def coefficients(rows, u, v, k, oc, coef, north):
    for r in chunks(rows):
        here, above = slice(r, r + CHUNK), slice(r + 1, r + CHUNK + 1)
        for h in range(2):
            face = 0.5 * (oc[h, here] * oc[h, above])
            na, nb = faces(v[h, here], v[h, above], k[h, here] + k[h, above], face)
            north[h, here] = na
            coef[3, h, here] = nb
    for r in chunks(rows):
        here, below = slice(r, r + CHUNK), slice(r - 1, r + CHUNK - 1)
        us, ks, os = ((x[0, here], x[1, here]) for x in (u, k, oc))
        ur, kr, orr = to_right(*us), to_right(*ks), to_right(*os)
        ea, eb = [], []
        for h in range(2):
            a, b = faces(us[h], ur[h], ks[h] + kr[h], 0.5 * (os[h] * orr[h]))
            ea.append(a)
            eb.append(b)
        wa, wb = to_left(*ea), to_left(*eb)
        for h in range(2):
            south = north[h, below]
            coef[0, h, here] = (1.0 - (ea[h] + wb[h])) - (north[h, here] + coef[3, h, below])
            coef[1, h, here] = eb[h]
            coef[2, h, here] = wa[h]
            coef[4, h, here] = south


def advance(rows, coef, q):
    for step in range(STEPS):
        src, dst = step % 2, (step + 1) % 2
        for r in chunks(rows):
            here = slice(r, r + CHUNK)
            c = [[coef[i, h, here] for h in range(2)] for i in range(5)]
            for i in range(NTR):
                mid = [q[src, i, h, here] for h in range(2)]
                right, left = to_right(*mid), to_left(*mid)
                for h in range(2):
                    up = q[src, i, h, r + 1 : r + CHUNK + 1]
                    down = q[src, i, h, r - 1 : r + CHUNK - 1]
                    q[dst, i, h, here] = (
                        c[0][h] * mid[h]
                        + c[1][h] * right[h]
                        + c[2][h] * left[h]
                        + c[3][h] * up
                        + c[4][h] * down
                    )


def field_scratch(rows):
    ext = (2, rows + 32, 128)
    return [
        pltpu.VMEM((4,) + ext, jnp.float32),
        pltpu.VMEM(ext, jnp.float32),
        pltpu.VMEM((5,) + ext, jnp.float32),
        pltpu.VMEM((2, NTR) + ext, jnp.float32),
    ]


def run_level(rows, level, t, v, m, o, fs, fn, fw, fe, vel, north, coef, q):
    even, odd = strips(fw, fe, level)
    for i in range(NTR):
        unpack_field(q.at[0, i], i, level, t, v, m, o, fs, fn, even, odd)
    for i in range(3):
        unpack_field(vel.at[i], NTR + i, level, t, v, m, o, fs, fn, even, odd)
    coefficients(rows, vel.at[0], vel.at[1], vel.at[2], vel.at[3], coef, north)
    advance(rows, coef, q)


def unpack_ocean(t, v, m, o, fs, fn, fw, fe, vel):
    even, odd = strips(fw, fe, 0)
    unpack_field(vel.at[3], FIELDS - 1, 0, t, v, m, o, fs, fn, even, odd)


def surface_kernel(
    order, accs, slot, t, v, m, o, fs, fn, fw, fe, w, out_q, out_send, out_keep,
    vel, north, coef, q, surf, *sums,
):
    rows = t.shape[2]
    unpack_ocean(t, v, m, o, fs, fn, fw, fe, vel)
    run_level(rows, 0, t, v, m, o, fs, fn, fw, fe, vel, north, coef, q)
    ocean = o[...].astype(jnp.float32)
    for i in range(NTR):
        done = q[0, i, 0, OFF : OFF + rows]
        out_q[i] = done
        surf[pl.ds(i, rows, stride=8), :] = done * ocean
    surf[pl.ds(NTR, rows, stride=8), :] = ocean
    for i in range(NTR + 1, 8):
        surf[pl.ds(i, rows, stride=8), :] = jnp.zeros((rows, 128), jnp.float32)
    for d in sums:
        d[...] = jnp.zeros_like(d)
    first = sub_ids(16) < 8
    kb = w.shape[1]

    def body(i, carry):
        s = surf[pl.ds(pl.multiple_of(16 * i, 16), 16), :]
        lhs = jnp.concatenate(
            [jnp.where(first, s, 0.0), jnp.where(first, 0.0, s)], axis=1
        ).astype(jnp.bfloat16)
        for k in range(0, kb, 2):
            rhs = jnp.concatenate(
                [
                    jnp.concatenate([w[2 * i + r, k], w[2 * i + r, k + 1]], axis=1)
                    for r in range(2)
                ],
                axis=0,
            )
            part = jnp.dot(lhs, rhs, preferred_element_type=jnp.float32)
            for r in range(2):
                for kk in range(2):
                    d = sums[(k + kk) % accs]
                    at = pl.ds(
                        pl.multiple_of(8 * slot[k + kk, 2 * i + r], 8), 8
                    )
                    d[at, :] += part[8 * r : 8 * r + 8, 128 * kk : 128 * kk + 128]
        return carry

    lax.fori_loop(0, rows // 2, body, 0, unroll=16)
    chunk = ABD * (NTR + 1)
    half = len(order) // 2
    for place, owner in enumerate(order):
        ref, base = (out_keep, place) if place < half else (out_send, place - half)
        for f in range(NTR + 1):
            total = sums[0][pl.ds(owner * ABD * 8 + f, ABD, stride=8), :]
            for d in sums[1:]:
                total = total + d[pl.ds(owner * ABD * 8 + f, ABD, stride=8), :]
            at = base * chunk + f * ABD
            ref[at : at + ABD, :] = total


def surface(order, slot, tracers, velocity, mixing, ocean, halo, weights):
    rows = tracers.shape[2]
    owners = len(order)
    accs = 4 if owners <= 32 else 1
    half = owners // 2 * ABD * (NTR + 1)
    return pl.pallas_call(
        functools.partial(surface_kernel, order, accs),
        in_specs=[pl.BlockSpec(memory_space=pltpu.SMEM)] + [WHOLE] * 9,
        out_specs=[WHOLE] * 3,
        scratch_shapes=field_scratch(rows)
        + [pltpu.VMEM((rows * 8, 128), jnp.float32)]
        + [pltpu.VMEM((owners * ABD * 8, 128), jnp.float32)] * accs,
        out_shape=[
            jax.ShapeDtypeStruct((NTR, rows, 128), jnp.float32),
            jax.ShapeDtypeStruct((half, 128), jnp.float32),
            jax.ShapeDtypeStruct((half, 128), jnp.float32),
        ],
        compiler_params=pltpu.CompilerParams(vmem_limit_bytes=22 << 20),
        cost_estimate=took(7),
        name="surface",
    )(slot, tracers, velocity, mixing, ocean, *halo, weights)


def deep_kernel(first, t, v, m, o, fs, fn, fw, fe, base, out, vel, north, coef, q):
    rows = t.shape[2]
    level = pl.program_id(0) + first

    @pl.when(pl.program_id(0) == 0)
    def _():
        unpack_ocean(t, v, m, o, fs, fn, fw, fe, vel)

    if first == 0:
        @pl.when(level == 0)
        def _():
            out[:, 0] = base[...]

    @pl.when(level > 0)
    def _():
        run_level(rows, level, t, v, m, o, fs, fn, fw, fe, vel, north, coef, q)
        for i in range(NTR):
            out[i, 0] = q[0, i, 0, OFF : OFF + rows]


def deep(tracers, velocity, mixing, ocean, halo, base, first, levels):
    rows = tracers.shape[2]
    return pl.pallas_call(
        functools.partial(deep_kernel, first),
        grid=(levels,),
        in_specs=[WHOLE] * 8 + [pl.BlockSpec(memory_space=pl.ANY) if first else WHOLE],
        out_specs=pl.BlockSpec((NTR, 1, rows, 128), lambda l: (0, l + first, 0, 0)),
        out_shape=jax.ShapeDtypeStruct(tracers.shape, jnp.float32),
        scratch_shapes=field_scratch(rows),
        input_output_aliases={8: 0} if first else {},
        compiler_params=pltpu.CompilerParams(vmem_limit_bytes=16 << 20),
        cost_estimate=took(1.8 * levels),
        name="deep",
    )(tracers, velocity, mixing, ocean, *halo, base)


def exchange_lat(to_south, to_north):
    n = lax.axis_size("gy")
    from_south = lax.ppermute(to_north, "gy", [(i, i + 1) for i in range(n - 1)])
    from_north = lax.ppermute(to_south, "gy", [(i + 1, i) for i in range(n - 1)])
    return from_south, from_north


def exchange_lon(to_west, to_east):
    n = lax.axis_size("gx")
    from_west = lax.ppermute(to_east, "gx", [(i, (i + 1) % n) for i in range(n)])
    from_east = lax.ppermute(to_west, "gx", [((i + 1) % n, i) for i in range(n)])
    return from_west, from_east


def partner(a, mask, n):
    return lax.ppermute(a, AXES, [(i, i ^ mask) for i in range(n)])


def rounds_of(owners):
    bits = owners.bit_length() - 1
    out, at = [(0, 1)], 1
    while at < bits:
        width = min(2, bits - at)
        out.append((at, width))
        at += width
    return out


def order_of(owners):
    def key(owner):
        return tuple((owner >> at) & ((1 << width) - 1) for at, width in rounds_of(owners))
    return sorted(range(owners), key=key)


def per_device(tracers, velocity, mixing, land_mask, remap_weights, remap_dest):
    owners = lax.axis_size("gx") * lax.axis_size("gy")
    levels = tracers.shape[1]
    me = lax.axis_index("gx") * lax.axis_size("gy") + lax.axis_index("gy")
    dest = remap_dest[:, 0].T
    slot = jnp.bitwise_xor(dest // ABD, me) * ABD + dest % ABD

    tile = (tracers, velocity, mixing, land_mask)
    lat = exchange_lat(*lat_pack(*tile))
    lat, slot = lax.optimization_barrier((lat, slot))
    to_west, to_east = lon_pack(*tile, *lat)
    lon = exchange_lon(to_west, to_east)
    weights = fetch(remap_weights, to_west)
    lon, weights = lax.optimization_barrier((lon, weights))

    order = order_of(owners)
    weights = pltpu.with_memory_space_constraint(weights, pltpu.VMEM)
    done, send, keep = surface(order, slot, *tile, lat + lon, weights)
    total = keep + partner(send, 1, owners)
    lon, total = lax.optimization_barrier((lon, total))
    values = done
    rounds = rounds_of(owners)[1:]
    cut = [0] + [levels * (i + 1) // len(rounds) for i in range(len(rounds))]
    cut[1:-1] = [c + 1 for c in cut[1:-1]]
    for i, (at, width) in enumerate(rounds):
        parts = total.reshape((1 << width, -1, 128))
        got = [partner(parts[j], j << at, owners) for j in range(1, 1 << width)]
        values = deep(*tile, lat + lon, values, cut[i], cut[i + 1] - cut[i])
        got, values = lax.optimization_barrier((got, values))
        total = parts[0]
        for g in got:
            total = total + g
    atmo = total.reshape(NTR + 1, ABD, 128).transpose(1, 0, 2)
    return values, atmo


def solution(mesh):
    placed = (
        P(None, None, "gy", "gx"),
        P(None, None, "gy", "gx"),
        P(None, "gy", "gx"),
        P("gy", "gx"),
        P("gy", None, "gx", None),
        P("gy", "gx", None),
    )
    return jax.shard_map(
        per_device,
        mesh=mesh,
        in_specs=placed,
        out_specs=(P(None, None, "gy", "gx"), P(("gx", "gy"), None, None)),
        check_vma=False,
    )
```

```python
import functools

import jax
import jax.numpy as jnp
from jax import lax
from jax.experimental import pallas as pl
from jax.experimental.pallas import tpu as pltpu
from jax.sharding import PartitionSpec as P

STEPS = 4
ABD = 16
NTR = 4
FIELDS = 8
OFF = 16
FIRST, SECOND = 3, 3
COUNT = 2
UNIT = 16
AXES = ("gx", "gy")


WHOLE = pl.BlockSpec(memory_space=pltpu.VMEM)
SCALARS = pl.BlockSpec(memory_space=pltpu.SMEM)


def took(us):
    return pl.CostEstimate(flops=0, bytes_accessed=int(us * 3.5e6), transcendentals=0)


def in_hbm(a):
    return pltpu.with_memory_space_constraint(a, pltpu.HBM)


def in_vmem(a):
    return pltpu.with_memory_space_constraint(a, pltpu.VMEM)


def lane_ids(rows):
    return lax.broadcasted_iota(jnp.int32, (rows, 128), 1)


def sub_ids(rows):
    return lax.broadcasted_iota(jnp.int32, (rows, 128), 0)


def parity(axis):
    return lax.axis_index(axis) & 1


def pick(odd, a, b):
    return jnp.where(odd == 0, a, b), jnp.where(odd == 0, b, a)


def lat_pack_kernel(tl, vl, ml, ol, th, vh, mh, oh, first_ref, second_ref):
    top = sub_ids(8) < 4
    for level in range(tl.shape[1]):

        def fields(t, v, m, o):
            out = [t[i, level] for i in range(NTR)] + [v[0, level], v[1, level], m[level]]
            out.append(o[...].astype(jnp.float32) if level == 0 else m[level])
            return out

        low, high = fields(tl, vl, ml, ol), fields(th, vh, mh, oh)
        for p in range(FIELDS // 2):
            here = slice(8 * p, 8 * p + 8)
            a, b = low[2 * p], low[2 * p + 1]
            south = jnp.where(top, a, pltpu.roll(b, 4, 0))
            a, b = high[2 * p], high[2 * p + 1]
            north = jnp.where(top, pltpu.roll(a, 4, 0), b)
            first_ref[level, here], second_ref[level, here] = pick(parity("gy"), north, south)


def lat_pack(tracers, velocity, mixing, ocean):
    levels, rows = tracers.shape[1:3]
    last = rows // 8 - 1

    def specs(block):
        return [
            pl.BlockSpec((NTR, levels, 8, 128), lambda l: (0, 0, block, 0)),
            pl.BlockSpec((2, levels, 8, 128), lambda l: (0, 0, block, 0)),
            pl.BlockSpec((levels, 8, 128), lambda l: (0, block, 0)),
            pl.BlockSpec((8, 128), lambda l: (block, 0)),
        ]

    arrays = [in_hbm(a) for a in (tracers, velocity, mixing, ocean)]
    strip = jax.ShapeDtypeStruct((levels, 32, 128), jnp.float32)
    return pl.pallas_call(
        lat_pack_kernel,
        grid=(1,),
        in_specs=specs(0) + specs(last),
        out_specs=[WHOLE] * 2,
        out_shape=[strip, strip],
        compiler_params=pltpu.CompilerParams(vmem_limit_bytes=4 << 20),
        cost_estimate=took(2),
        name="lat_pack",
    )(*arrays, *arrays)


def field_index(f, level, levels):
    return (FIELDS - 1) * levels if f == FIELDS - 1 else f * levels + level


def tile_copies(levels, t, v, m, o, out, mask, sems):
    sources = [t.at[i] for i in range(NTR)] + [v.at[0], v.at[1], m]
    copies = [pltpu.make_async_copy(o, mask, sems.at[FIELDS - 1])]
    for f, source in enumerate(sources):
        target = out.at[pl.ds(f * levels, levels)]
        copies.append(pltpu.make_async_copy(source.at[pl.ds(0, levels)], target, sems.at[f]))
    return copies


def tile_shape(levels, rows):
    return ((FIELDS - 1) * levels + 1, rows, 128)


def finish_tile(copies, out, mask):
    for copy in copies:
        copy.wait()
    out[out.shape[0] - 1] = mask[...].astype(jnp.float32)


def lat_halo_blocks(lat, f, level):
    first, second = lat
    p, odd = f // 2, f % 2
    here = slice(8 * p, 8 * p + 8)
    n, s = pick(parity("gy"), first[level, here], second[level, here])
    if odd:
        return s, pltpu.roll(n, 4, 0)
    return pltpu.roll(s, 4, 0), n


def one_hot(ref, rows, cols, match):
    i, j = sub_ids(128), lane_ids(128)
    for r in range(0, rows, 128):
        for c in range(0, cols, 128):
            hit = match(i, j, r // 128, c // 128)
            ref[r : r + 128, c : c + 128] = jnp.where(hit, 1.0, 0.0).astype(jnp.bfloat16)


def own_match(i, j):
    s = j & 31
    return ((s < 8) & (i == s + 120)) | ((s >= 16) & (s < 24) & (i == s - 16))


def strip_match(i, j, f):
    s = j & 31
    west = (s >= 12) & (s < 16) & (i == 4 * f + s - 12)
    east = (s >= 8) & (s < 12) & (i == 4 * f + 4 + s - 8)
    return west | east


def tables_kernel(own_q, own, strip, back):
    one_hot(own_q, NTR * 128, 128, lambda i, j, r, c: own_match(i, j) & ((j >> 5) == r))
    one_hot(own, 128, 128, lambda i, j, r, c: own_match(i, j))

    def strips(i, j, odd, c):
        if c > 0:
            f = NTR + c - 1
            if f % 2 != odd:
                return i < 0
            return strip_match(i, j, f)
        hit = i < 0
        for f in range(odd, NTR, 2):
            hit |= strip_match(i, j, f) & ((j >> 5) == f)
        return hit

    one_hot(strip, strip.shape[0], strip.shape[1], strips)
    one_hot(
        back,
        128,
        NTR * 128,
        lambda i, j, r, c: (i == 32 * c + 16 + j) & (j < 4)
        | (i == 32 * c + 4 + j - 124) & (j >= 124),
    )


TABLES = [(NTR * 128, 128), (128, 128), (256, 5 * 128), (128, NTR * 128)]


def unit_place(n):
    return UNIT * (n // 4), 32 * (n % 4)


def strip_rows(count, rows):
    return UNIT * ((count * ((rows + 16) // UNIT) + 3) // 4)


def pack_columns(first, levels, x, lat, first_ref, second_ref, count):
    units = (x.shape[1] + 16) // UNIT
    lane = lane_ids(UNIT)
    west = east = jnp.zeros((UNIT, 128), jnp.float32)
    for l in range(count):
        level = first + l
        fields = range(FIELDS if level == 0 else FIELDS - 1)
        whole = []
        for f in fields:
            s, n = lat_halo_blocks(lat, f, level)
            whole.append(jnp.concatenate([s, x[field_index(f, level, levels)], n], axis=0))
        for r in range(units):
            place, base = unit_place(l * units + r)
            for f in fields:
                at = base + 4 * f
                turned = pltpu.roll(whole[f][UNIT * r : UNIT * r + UNIT], (at - 124) % 128, 1)
                east = jnp.where((lane >= at) & (lane < at + 4), turned, east)
                to = (at + 4) % 128
                west = jnp.where((lane >= to) & (lane < to + 4), turned, west)
            if base == 96 or (l == count - 1 and r == units - 1):
                here = slice(place, place + UNIT)
                first_ref[here], second_ref[here] = pick(parity("gx"), east, west)
                west = east = jnp.zeros((UNIT, 128), jnp.float32)


def fetch_kernel(after, t, v, m, o, w, x, out, mask, sems, sem):
    copies = tile_copies(t.shape[1], t, v, m, o, x, mask, sems)
    copies.append(pltpu.make_async_copy(w.at[pl.ds(0, out.shape[0])], out, sem))
    for copy in copies:
        copy.start()
    finish_tile(copies[:-1], x, mask)
    copies[-1].wait()


def fetch(after, arrays, weights):
    levels, rows = arrays[0].shape[1:3]
    part = (rows * FIRST // 8,) + weights.shape[1:]
    return pl.pallas_call(
        fetch_kernel,
        in_specs=[pl.BlockSpec(memory_space=pl.ANY)]
        + [pl.BlockSpec(memory_space=pltpu.HBM)] * 5,
        out_specs=[WHOLE] * 2,
        out_shape=[
            pltpu.VMEM(tile_shape(levels, rows), jnp.float32),
            pltpu.VMEM(part, weights.dtype),
        ],
        scratch_shapes=[
            pltpu.VMEM(arrays[3].shape, jnp.int32),
            pltpu.SemaphoreType.DMA((FIELDS,)),
            pltpu.SemaphoreType.DMA,
        ],
        compiler_params=pltpu.CompilerParams(vmem_limit_bytes=2 << 20),
        cost_estimate=took(3),
        name="fetch",
    )(after, *(in_hbm(a) for a in (*arrays, weights)))


def lon_pack_kernel(levels, la, lb, x, first_ref, second_ref):
    pack_columns(0, levels, x, (la, lb), first_ref, second_ref, 1)


def others_pack_kernel(levels, skip, la, lb, x, w, first_ref, second_ref, *refs):
    out, own_q, own, strip, back, sem = refs
    copy = pltpu.make_async_copy(w.at[pl.ds(skip, out.shape[0])], out, sem)
    copy.start()
    pack_columns(1, levels, x, (la, lb), first_ref, second_ref, levels - 1)
    tables_kernel(own_q, own, strip, back)
    copy.wait()


def lon_pack(lat, tile, levels, weights=None):
    rows = tile.shape[1]
    count = levels - 1 if weights is not None else 1
    out = [jax.ShapeDtypeStruct((strip_rows(count, rows), 128), jnp.float32)] * 2
    if weights is None:
        kernel = functools.partial(lon_pack_kernel, levels)
    else:
        kernel = functools.partial(others_pack_kernel, levels, rows * FIRST // 8)
        out.append(pltpu.VMEM((rows * SECOND // 8,) + weights.shape[1:], weights.dtype))
        out += [pltpu.VMEM(shape, jnp.bfloat16) for shape in TABLES]
    more = [] if weights is None else [in_hbm(weights)]
    return pl.pallas_call(
        kernel,
        in_specs=[WHOLE] * 3 + [pl.BlockSpec(memory_space=pltpu.HBM)] * len(more),
        out_specs=[WHOLE] * len(out),
        out_shape=out,
        scratch_shapes=[pltpu.SemaphoreType.DMA] * len(more),
        compiler_params=pltpu.CompilerParams(vmem_limit_bytes=4 << 20),
        cost_estimate=took(0.3 if weights is None else 2),
        name="lon_pack",
    )(*lat, in_vmem(tile), *more)


def unpack_field(ext, f, level, levels, x, lat):
    rows = x.shape[1]
    s, n = lat_halo_blocks(lat, f, level)
    ext[OFF - 8 : OFF] = s
    ext[OFF : OFF + rows] = x[field_index(f, level, levels)]
    ext[OFF + rows : OFF + rows + 8] = n


def terms(x, count):
    out = []
    for i in range(count):
        out.append(x.astype(jnp.bfloat16))
        if i < count - 1:
            x = x - out[-1].astype(jnp.float32)
    return out


def moved(parts, table, count):
    n = parts[0].shape[0]
    split = [terms(p, count) for p in parts]
    lhs = jnp.concatenate(
        [jnp.concatenate([p[i] for p in split], axis=1) for i in range(count)], axis=0
    )
    out = jnp.dot(lhs, table, preferred_element_type=jnp.float32)
    total = out[:n]
    for i in range(1, count):
        total = total + out[i * n : i * n + n]
    return total


def strip_parts(lon, level, units):
    near = lane_ids(UNIT) % 8 < 4
    first, second, base = lon
    even, odd = [], []
    for r in range(units):
        row, lane = level_unit(level - base, r, units)
        here = pl.ds(row, UNIT)
        e, w = pick(parity("gx"), first[here, :], second[here, :])
        even.append(pltpu.roll(jnp.where(near, w, e), (128 - lane) & 127, 1))
        odd.append(pltpu.roll(jnp.where(near, e, w), (128 - lane) & 127, 1))
    return [jnp.concatenate(even, axis=0), jnp.concatenate(odd, axis=0)]


def level_unit(l, r, units):
    n = l * units + r
    if isinstance(n, int):
        return unit_place(n)
    return pl.multiple_of(UNIT * (n >> 2), UNIT), 32 * (n & 3)


def side_arrays(rows, level, fields, sides, columns, lon, own, strip, count):
    body = slice(OFF - 8, OFF + rows + 8)
    packed = strip_parts(lon, level, (rows + 16) // UNIT)
    first, last = 128 * columns[0], 128 * (columns[-1] + 1)
    got = moved(packed, strip[:, first:last], count)
    for i, (parts, side, table) in enumerate(zip(fields, sides, own)):
        mine = moved([p[body] for p in parts], table[...], count)
        side[body] = mine + got[:, 128 * i : 128 * i + 128]


def to_right(a):
    return pltpu.roll(a, 127, 1)


def to_left(a):
    return pltpu.roll(a, 1, 1)


def chunks(first, last, size):
    return [slice(r, r + size) for r in range(first, last, size)]


def around(rows):
    return chunks(OFF - 8, OFF + rows + 8, 24)


def moved_rows(here, by):
    return slice(here.start + by, here.stop + by)


def open_faces(rows, ocean, east, north):
    for here in around(rows):
        o = ocean[here]
        east[here] = 0.5 * (o * to_right(o))
        north[here] = 0.5 * (o * ocean[moved_rows(here, 1)])


def faces(a, b, mix, face):
    vel = a + b
    low = jnp.maximum(vel, 0.0) + mix
    return face * low, face * (low - vel)


def coefficients(rows, u, v, k, east, north, coef, above):
    for here in around(rows):
        up = moved_rows(here, 1)
        a, b = faces(v[here], v[up], k[here] + k[up], north[here])
        above[here] = a
        coef[3, here] = b
    for here in around(rows):
        below = moved_rows(here, -1)
        us, ks = u[here], k[here]
        a, b = faces(us, to_right(us), ks + to_right(ks), east[here])
        wa, wb = to_left(a), to_left(b)
        south = above[below]
        coef[0, here] = (1.0 - (a + wb)) - (above[here] + coef[3, below])
        coef[1, here] = b
        coef[2, here] = wa
        coef[4, here] = south


def stencil(c, q, here):
    mid = q[here]
    return (
        c[0] * mid
        + c[1] * to_right(mid)
        + c[2] * to_left(mid)
        + c[3] * q[moved_rows(here, 1)]
        + c[4] * q[moved_rows(here, -1)]
    )


def advance(rows, coef, side_coef, q, side):
    for step in range(STEPS):
        src, dst = step % 2, (step + 1) % 2
        last = step == STEPS - 1
        for here in chunks(OFF, OFF + rows, 32) if last else around(rows):
            c = [side_coef[i, here] for i in range(5)]
            side[dst, here] = stencil(c, side.at[src], here)
            c = [coef[i, here] for i in range(5)]
            for i in range(NTR):
                q[dst, i, here] = stencil(c, q.at[src, i], here)


def field_scratch(rows):
    ext = (rows + 32, 128)
    return [
        pltpu.VMEM((count,) + ext, jnp.float32)
        for count in (3, 3, 4, 2, 5, 5)
    ] + [
        pltpu.VMEM((2, NTR) + ext, jnp.float32),
        pltpu.VMEM((2,) + ext, jnp.float32),
    ]


def set_faces(x, levels, lat, lon, tables, scratch):
    rows = x.shape[1]
    own_q, own, strip, back = tables
    vel, side_vel, face = scratch[:3]
    ocean, side = vel.at[0], side_vel.at[0]
    unpack_field(ocean, FIELDS - 1, 0, levels, x, lat)
    side_arrays(rows, 0, [[ocean]], [side], [NTR], lon, [own], strip, 1)
    open_faces(rows, ocean, face.at[0], face.at[1])
    open_faces(rows, side, face.at[2], face.at[3])


def run_level(level, x, levels, lat, lon, tables, scratch, count):
    rows = x.shape[1]
    own_q, own, strip, back = tables
    vel, side_vel, face, above, coef, side_coef, q, side = scratch
    now = [q.at[0, i] for i in range(NTR)]
    three = [vel.at[i] for i in range(3)]
    for i, ref in enumerate(now + three):
        unpack_field(ref, i, level, levels, x, lat)
    side_arrays(
        rows,
        level,
        [now] + [[ref] for ref in three],
        [side.at[0]] + [side_vel.at[i] for i in range(3)],
        range(NTR),
        lon,
        [own_q, own, own, own],
        strip,
        count,
    )
    coefficients(rows, *three, face.at[0], face.at[1], coef, above.at[0])
    coefficients(
        rows, *(side_vel.at[i] for i in range(3)), face.at[2], face.at[3], side_coef, above.at[1]
    )
    advance(rows, coef, side_coef, q, side)
    body = slice(OFF, OFF + rows)
    ends = moved([side[0, body]], back[...], count)
    lane = lane_ids(rows)
    inner = (lane >= STEPS) & (lane < 128 - STEPS)
    return [
        jnp.where(inner, q[0, i, body], ends[:, 128 * i : 128 * i + 128]) for i in range(NTR)
    ]


def surface_kernel(order, accs, levels, slot, x, la, lb, wa, wb, *refs):
    tables, w_held, w_more, w_hbm = refs[:4], refs[4], refs[5], refs[6]
    out_q, out_send, out_keep = refs[7:10]
    scratch, surf, w_last, sem, sums = refs[10:18], refs[18], refs[19], refs[20], refs[21:]
    rows = x.shape[1]
    done_rows = w_held.shape[0] + w_more.shape[0]
    copy = pltpu.make_async_copy(w_hbm.at[pl.ds(done_rows, w_last.shape[0])], w_last, sem)
    copy.start()
    lat, lon = (la, lb), (wa, wb, 0)
    set_faces(x, levels, lat, lon, tables, scratch)
    ocean = x[field_index(FIELDS - 1, 0, levels)]
    for i, done in enumerate(run_level(0, x, levels, lat, lon, tables, scratch, 3)):
        out_q[i] = done
        surf[pl.ds(i, rows, stride=8), :] = done * ocean
    surf[pl.ds(NTR, rows, stride=8), :] = ocean
    for i in range(NTR + 1, 8):
        surf[pl.ds(i, rows, stride=8), :] = jnp.zeros((rows, 128), jnp.float32)
    for d in sums:
        d[...] = jnp.zeros_like(d)
    first = sub_ids(16) < 8
    kb = w_held.shape[1]

    def body(w, base, j, carry):
        i = j + base
        s = surf[pl.ds(pl.multiple_of(16 * i, 16), 16), :]
        lhs = jnp.concatenate(
            [jnp.where(first, s, 0.0), jnp.where(first, 0.0, s)], axis=1
        ).astype(jnp.bfloat16)
        for k in range(0, kb, 2):
            rhs = jnp.concatenate(
                [
                    jnp.concatenate([w[2 * j + r, k], w[2 * j + r, k + 1]], axis=1)
                    for r in range(2)
                ],
                axis=0,
            )
            part = jnp.dot(lhs, rhs, preferred_element_type=jnp.float32)
            for r in range(2):
                for kk in range(2):
                    d = sums[(k + kk) % accs]
                    at = pl.ds(
                        pl.multiple_of(8 * slot[k + kk, 2 * i + r], 8), 8
                    )
                    d[at, :] += part[8 * r : 8 * r + 8, 128 * kk : 128 * kk + 128]
        return carry

    start = 0
    for w in (w_held, w_more, w_last):
        if w is w_last:
            copy.wait()
        pairs = w.shape[0] // 2
        lax.fori_loop(0, pairs, functools.partial(body, w, start), 0, unroll=8)
        start += pairs
    chunk = ABD * (NTR + 1)
    half = len(order) // 2
    for place, owner in enumerate(order):
        ref, base = (out_keep, place) if place < half else (out_send, place - half)
        for f in range(NTR + 1):
            total = sums[0][pl.ds(owner * ABD * 8 + f, ABD, stride=8), :]
            for d in sums[1:]:
                total = total + d[pl.ds(owner * ABD * 8 + f, ABD, stride=8), :]
            at = base * chunk + f * ABD
            ref[at : at + ABD, :] = total


def surface(order, slot, tile, levels, lat, lon, tables, held, weights):
    rows = tile.shape[1]
    owners = len(order)
    accs = 2 if owners <= 32 else 1
    half = owners // 2 * ABD * (NTR + 1)
    last = (rows - sum(w.shape[0] for w in held),) + weights.shape[1:]
    return pl.pallas_call(
        functools.partial(surface_kernel, order, accs, levels),
        in_specs=[SCALARS] + [WHOLE] * 11 + [pl.BlockSpec(memory_space=pltpu.HBM)],
        out_specs=[WHOLE] * 3,
        scratch_shapes=field_scratch(rows)
        + [pltpu.VMEM((rows * 8, 128), jnp.float32)]
        + [pltpu.VMEM(last, weights.dtype), pltpu.SemaphoreType.DMA]
        + [pltpu.VMEM((owners * ABD * 8, 128), jnp.float32)] * accs,
        out_shape=[
            jax.ShapeDtypeStruct((NTR, rows, 128), jnp.float32),
            jax.ShapeDtypeStruct((half, 128), jnp.float32),
            jax.ShapeDtypeStruct((half, 128), jnp.float32),
        ],
        compiler_params=pltpu.CompilerParams(vmem_limit_bytes=24 << 20),
        cost_estimate=took(7),
        name="surface",
    )(slot, in_vmem(tile), *lat, *lon, *tables, *(in_vmem(w) for w in held), in_hbm(weights))


def deep_kernel(first, levels, x, la, lb, oa, ob, wa, wb, *refs):
    tables, base, out, scratch = refs[:4], refs[4], refs[5], refs[6:]
    lat = (la, lb)
    level = pl.program_id(0) + first

    @pl.when(pl.program_id(0) == 0)
    def _():
        set_faces(x, levels, lat, (oa, ob, 0), tables, scratch)

    if first == 0:
        @pl.when(level == 0)
        def _():
            out[:, 0] = base[...]

    @pl.when(level > 0)
    def _():
        lon = (wa, wb, 1)
        for i, done in enumerate(run_level(level, x, levels, lat, lon, tables, scratch, COUNT)):
            out[i, 0] = done


def deep(tile, levels, lat, lon0, lon, tables, base, first, count):
    rows = tile.shape[1]
    return pl.pallas_call(
        functools.partial(deep_kernel, first, levels),
        grid=(count,),
        in_specs=[WHOLE] * 11 + [pl.BlockSpec(memory_space=pl.ANY) if first else WHOLE],
        out_specs=pl.BlockSpec((NTR, 1, rows, 128), lambda l: (0, l + first, 0, 0)),
        out_shape=jax.ShapeDtypeStruct((NTR, levels, rows, 128), jnp.float32),
        scratch_shapes=field_scratch(rows),
        input_output_aliases={11: 0} if first else {},
        compiler_params=pltpu.CompilerParams(vmem_limit_bytes=16 << 20),
        cost_estimate=took(1.3 * count),
        name="deep",
    )(in_vmem(tile), *lat, *lon0, *lon, *tables, base)


def swap(first, second, axis, ring):
    n = lax.axis_size(axis)
    even = [(i, i + 1) for i in range(0, n - 1, 2)]
    odd = [(i, (i + 1) % n) for i in range(1, n if ring else n - 1, 2)]
    second = lax.ppermute(second, axis, odd + [(j, i) for i, j in odd])
    first = lax.ppermute(first, axis, even + [(j, i) for i, j in even])
    return first, second


def partner(a, mask, n):
    return lax.ppermute(a, AXES, [(i, i ^ mask) for i in range(n)])


def rounds_of(owners):
    bits = owners.bit_length() - 1
    out, at = [(0, 1)], 1
    while at < bits:
        width = min(2, bits - at)
        out.append((at, width))
        at += width
    return out


def order_of(owners):
    def key(owner):
        return tuple((owner >> at) & ((1 << width) - 1) for at, width in rounds_of(owners))
    return sorted(range(owners), key=key)


def per_device(tracers, velocity, mixing, land_mask, remap_weights, remap_dest):
    owners = lax.axis_size("gx") * lax.axis_size("gy")
    levels = tracers.shape[1]
    me = lax.axis_index("gx") * lax.axis_size("gy") + lax.axis_index("gy")
    dest = remap_dest[:, 0].T
    slot = jnp.bitwise_xor(dest // ABD, me) * ABD + dest % ABD

    arrays = (tracers, velocity, mixing, land_mask)
    strips = lat_pack(*arrays)
    lat = swap(*strips, "gy", False)
    slot, first = lax.optimization_barrier((slot, strips[0]))
    tile, held = fetch(slot, arrays, remap_weights)
    lat, tile, held = lax.optimization_barrier((lat, tile, held))
    first, second = lon_pack(lat, tile, levels)
    lon0 = swap(first, second, "gx", True)
    lat, first = lax.optimization_barrier((lat, first))
    first, second, more, *tables = lon_pack(lat, tile, levels, remap_weights)
    lon0, first, more, tables = lax.optimization_barrier((lon0, first, more, tables))
    lon = swap(first, second, "gx", True)

    order = order_of(owners)
    done, send, keep = surface(
        order, slot, tile, levels, lat, lon0, tables, (held, more), remap_weights
    )
    lon, send = lax.optimization_barrier((lon, send))
    total = keep + partner(send, 1, owners)
    lon, total = lax.optimization_barrier((lon, total))
    values = done
    rounds = rounds_of(owners)[1:]
    cut = [0] + [levels * 3 * (i + 1) // (3 * len(rounds) - 2) for i in range(len(rounds) - 1)]
    cut.append(levels)
    for i, (at, width) in enumerate(rounds):
        parts = total.reshape((1 << width, -1, 128))
        got = [partner(parts[j], j << at, owners) for j in range(1, 1 << width)]
        values = deep(
            tile, levels, lat, lon0, lon, tables, values, cut[i], cut[i + 1] - cut[i]
        )
        got, values = lax.optimization_barrier((got, values))
        total = parts[0]
        for g in got:
            total = total + g
    atmo = total.reshape(NTR + 1, ABD, 128).transpose(1, 0, 2)
    return values, atmo


def solution(mesh):
    placed = (
        P(None, None, "gy", "gx"),
        P(None, None, "gy", "gx"),
        P(None, "gy", "gx"),
        P("gy", "gx"),
        P("gy", None, "gx", None),
        P("gy", "gx", None),
    )
    return jax.shard_map(
        per_device,
        mesh=mesh,
        in_specs=placed,
        out_specs=(P(None, None, "gy", "gx"), P(("gx", "gy"), None, None)),
        check_vma=False,
    )
```

```python
import functools

import jax
import jax.numpy as jnp
from jax import lax
from jax.experimental import pallas as pl
from jax.experimental.pallas import tpu as pltpu
from jax.sharding import PartitionSpec as P

STEPS = 4
ABD = 16
NTR = 4
FIELDS = 8
OFF = 16
FIRST, SECOND = 3, 3
COUNT = 2
UNIT = 16
AXES = ("gx", "gy")


WHOLE = pl.BlockSpec(memory_space=pltpu.VMEM)
SCALARS = pl.BlockSpec(memory_space=pltpu.SMEM)


def took(us):
    return pl.CostEstimate(flops=0, bytes_accessed=int(us * 3.5e6), transcendentals=0)


def in_hbm(a):
    return pltpu.with_memory_space_constraint(a, pltpu.HBM)


def in_vmem(a):
    return pltpu.with_memory_space_constraint(a, pltpu.VMEM)


def lane_ids(rows):
    return lax.broadcasted_iota(jnp.int32, (rows, 128), 1)


def sub_ids(rows):
    return lax.broadcasted_iota(jnp.int32, (rows, 128), 0)


def parity(axis):
    return lax.axis_index(axis) & 1


def pick(odd, a, b):
    return jnp.where(odd == 0, a, b), jnp.where(odd == 0, b, a)


def lat_pack_kernel(tl, vl, ml, ol, th, vh, mh, oh, first_ref, second_ref):
    top = sub_ids(8) < 4
    for level in range(tl.shape[1]):

        def fields(t, v, m, o):
            out = [t[i, level] for i in range(NTR)] + [v[0, level], v[1, level], m[level]]
            out.append(o[...].astype(jnp.float32) if level == 0 else m[level])
            return out

        low, high = fields(tl, vl, ml, ol), fields(th, vh, mh, oh)
        for p in range(FIELDS // 2):
            here = slice(8 * p, 8 * p + 8)
            a, b = low[2 * p], low[2 * p + 1]
            south = jnp.where(top, a, pltpu.roll(b, 4, 0))
            a, b = high[2 * p], high[2 * p + 1]
            north = jnp.where(top, pltpu.roll(a, 4, 0), b)
            first_ref[level, here], second_ref[level, here] = pick(parity("gy"), north, south)


def lat_pack(tracers, velocity, mixing, ocean):
    levels, rows = tracers.shape[1:3]
    last = rows // 8 - 1

    def specs(block):
        return [
            pl.BlockSpec((NTR, levels, 8, 128), lambda l: (0, 0, block, 0)),
            pl.BlockSpec((2, levels, 8, 128), lambda l: (0, 0, block, 0)),
            pl.BlockSpec((levels, 8, 128), lambda l: (0, block, 0)),
            pl.BlockSpec((8, 128), lambda l: (block, 0)),
        ]

    arrays = [in_hbm(a) for a in (tracers, velocity, mixing, ocean)]
    strip = jax.ShapeDtypeStruct((levels, 32, 128), jnp.float32)
    return pl.pallas_call(
        lat_pack_kernel,
        grid=(1,),
        in_specs=specs(0) + specs(last),
        out_specs=[WHOLE] * 2,
        out_shape=[strip, strip],
        compiler_params=pltpu.CompilerParams(vmem_limit_bytes=4 << 20),
        cost_estimate=took(2),
        name="lat_pack",
    )(*arrays, *arrays)


def field_index(f, level, levels):
    return (FIELDS - 1) * levels if f == FIELDS - 1 else f * levels + level


def tile_copies(levels, t, v, m, o, out, mask, sems):
    sources = [t.at[i] for i in range(NTR)] + [v.at[0], v.at[1], m]
    copies = [pltpu.make_async_copy(o, mask, sems.at[FIELDS - 1])]
    for f, source in enumerate(sources):
        target = out.at[pl.ds(f * levels, levels)]
        copies.append(pltpu.make_async_copy(source.at[pl.ds(0, levels)], target, sems.at[f]))
    return copies


def tile_shape(levels, rows):
    return ((FIELDS - 1) * levels + 1, rows, 128)


def finish_tile(copies, out, mask):
    for copy in copies:
        copy.wait()
    out[out.shape[0] - 1] = mask[...].astype(jnp.float32)


def lat_halo_blocks(lat, f, level):
    first, second = lat
    p, odd = f // 2, f % 2
    here = slice(8 * p, 8 * p + 8)
    n, s = pick(parity("gy"), first[level, here], second[level, here])
    if odd:
        return s, pltpu.roll(n, 4, 0)
    return pltpu.roll(s, 4, 0), n


def one_hot(ref, rows, cols, match):
    i, j = sub_ids(128), lane_ids(128)
    for r in range(0, rows, 128):
        for c in range(0, cols, 128):
            hit = match(i, j, r // 128, c // 128)
            ref[r : r + 128, c : c + 128] = jnp.where(hit, 1.0, 0.0).astype(jnp.bfloat16)


def own_match(i, j):
    s = j & 31
    return ((s < 8) & (i == s + 120)) | ((s >= 16) & (s < 24) & (i == s - 16))


def strip_match(i, j, f):
    s = j & 31
    west = (s >= 12) & (s < 16) & (i == 4 * f + s - 12)
    east = (s >= 8) & (s < 12) & (i == 4 * f + 4 + s - 8)
    return west | east


def tables_kernel(own_q, own, strip, back):
    one_hot(own_q, NTR * 128, 128, lambda i, j, r, c: own_match(i, j) & ((j >> 5) == r))
    one_hot(own, 128, 128, lambda i, j, r, c: own_match(i, j))

    def strips(i, j, odd, c):
        if c > 0:
            f = NTR + c - 1
            if f % 2 != odd:
                return i < 0
            return strip_match(i, j, f)
        hit = i < 0
        for f in range(odd, NTR, 2):
            hit |= strip_match(i, j, f) & ((j >> 5) == f)
        return hit

    one_hot(strip, strip.shape[0], strip.shape[1], strips)
    one_hot(
        back,
        128,
        NTR * 128,
        lambda i, j, r, c: (i == 32 * c + 16 + j) & (j < 4)
        | (i == 32 * c + 4 + j - 124) & (j >= 124),
    )


TABLES = [(NTR * 128, 128), (128, 128), (256, 5 * 128), (128, NTR * 128)]


def unit_place(n):
    return UNIT * (n // 4), 32 * (n % 4)


def strip_rows(count, rows):
    return UNIT * ((count * ((rows + 16) // UNIT) + 3) // 4)


def pack_columns(first, levels, x, lat, first_ref, second_ref, count):
    units = (x.shape[1] + 16) // UNIT
    lane = lane_ids(UNIT)
    west = east = jnp.zeros((UNIT, 128), jnp.float32)
    for l in range(count):
        level = first + l
        fields = range(FIELDS if level == 0 else FIELDS - 1)
        whole = []
        for f in fields:
            s, n = lat_halo_blocks(lat, f, level)
            whole.append(jnp.concatenate([s, x[field_index(f, level, levels)], n], axis=0))
        for r in range(units):
            place, base = unit_place(l * units + r)
            for f in fields:
                at = base + 4 * f
                turned = pltpu.roll(whole[f][UNIT * r : UNIT * r + UNIT], (at - 124) % 128, 1)
                east = jnp.where((lane >= at) & (lane < at + 4), turned, east)
                to = (at + 4) % 128
                west = jnp.where((lane >= to) & (lane < to + 4), turned, west)
            if base == 96 or (l == count - 1 and r == units - 1):
                here = slice(place, place + UNIT)
                first_ref[here], second_ref[here] = pick(parity("gx"), east, west)
                west = east = jnp.zeros((UNIT, 128), jnp.float32)


def fetch_kernel(after, t, v, m, o, w, x, out, mask, sems, sem):
    copies = tile_copies(t.shape[1], t, v, m, o, x, mask, sems)
    copies.append(pltpu.make_async_copy(w.at[pl.ds(0, out.shape[0])], out, sem))
    for copy in copies:
        copy.start()
    finish_tile(copies[:-1], x, mask)
    copies[-1].wait()


def fetch(after, arrays, weights):
    levels, rows = arrays[0].shape[1:3]
    part = (rows * FIRST // 8,) + weights.shape[1:]
    return pl.pallas_call(
        fetch_kernel,
        in_specs=[pl.BlockSpec(memory_space=pl.ANY)]
        + [pl.BlockSpec(memory_space=pltpu.HBM)] * 5,
        out_specs=[WHOLE] * 2,
        out_shape=[
            pltpu.VMEM(tile_shape(levels, rows), jnp.float32),
            pltpu.VMEM(part, weights.dtype),
        ],
        scratch_shapes=[
            pltpu.VMEM(arrays[3].shape, jnp.int32),
            pltpu.SemaphoreType.DMA((FIELDS,)),
            pltpu.SemaphoreType.DMA,
        ],
        compiler_params=pltpu.CompilerParams(vmem_limit_bytes=2 << 20),
        cost_estimate=took(3),
        name="fetch",
    )(after, *(in_hbm(a) for a in (*arrays, weights)))


def lon_pack_kernel(levels, la, lb, x, first_ref, second_ref):
    pack_columns(0, levels, x, (la, lb), first_ref, second_ref, 1)


def others_pack_kernel(levels, skip, la, lb, x, w, first_ref, second_ref, *refs):
    out, own_q, own, strip, back, sem = refs
    copy = pltpu.make_async_copy(w.at[pl.ds(skip, out.shape[0])], out, sem)
    copy.start()
    pack_columns(1, levels, x, (la, lb), first_ref, second_ref, levels - 1)
    tables_kernel(own_q, own, strip, back)
    copy.wait()


def lon_pack(lat, tile, levels, weights=None):
    rows = tile.shape[1]
    count = levels - 1 if weights is not None else 1
    out = [jax.ShapeDtypeStruct((strip_rows(count, rows), 128), jnp.float32)] * 2
    if weights is None:
        kernel = functools.partial(lon_pack_kernel, levels)
    else:
        kernel = functools.partial(others_pack_kernel, levels, rows * FIRST // 8)
        out.append(pltpu.VMEM((rows * SECOND // 8,) + weights.shape[1:], weights.dtype))
        out += [pltpu.VMEM(shape, jnp.bfloat16) for shape in TABLES]
    more = [] if weights is None else [in_hbm(weights)]
    return pl.pallas_call(
        kernel,
        in_specs=[WHOLE] * 3 + [pl.BlockSpec(memory_space=pltpu.HBM)] * len(more),
        out_specs=[WHOLE] * len(out),
        out_shape=out,
        scratch_shapes=[pltpu.SemaphoreType.DMA] * len(more),
        compiler_params=pltpu.CompilerParams(vmem_limit_bytes=4 << 20),
        cost_estimate=took(0.3 if weights is None else 2),
        name="lon_pack",
    )(*lat, in_vmem(tile), *more)


def unpack_field(ext, f, level, levels, x, lat):
    rows = x.shape[1]
    s, n = lat_halo_blocks(lat, f, level)
    ext[OFF - 8 : OFF] = s
    ext[OFF : OFF + rows] = x[field_index(f, level, levels)]
    ext[OFF + rows : OFF + rows + 8] = n


def terms(x, count):
    out = []
    for i in range(count):
        out.append(x.astype(jnp.bfloat16))
        if i < count - 1:
            x = x - out[-1].astype(jnp.float32)
    return out


def moved(parts, table, count):
    n = parts[0].shape[0]
    split = [terms(p, count) for p in parts]
    lhs = jnp.concatenate(
        [jnp.concatenate([p[i] for p in split], axis=1) for i in range(count)], axis=0
    )
    out = jnp.dot(lhs, table, preferred_element_type=jnp.float32)
    total = out[:n]
    for i in range(1, count):
        total = total + out[i * n : i * n + n]
    return total


def strip_parts(lon, level, units):
    near = lane_ids(UNIT) % 8 < 4
    first, second, base = lon
    even, odd = [], []
    for r in range(units):
        row, lane = level_unit(level - base, r, units)
        here = pl.ds(row, UNIT)
        e, w = pick(parity("gx"), first[here, :], second[here, :])
        even.append(pltpu.roll(jnp.where(near, w, e), (128 - lane) & 127, 1))
        odd.append(pltpu.roll(jnp.where(near, e, w), (128 - lane) & 127, 1))
    return [jnp.concatenate(even, axis=0), jnp.concatenate(odd, axis=0)]


def level_unit(l, r, units):
    n = l * units + r
    if isinstance(n, int):
        return unit_place(n)
    return pl.multiple_of(UNIT * (n >> 2), UNIT), 32 * (n & 3)


def side_arrays(rows, level, fields, sides, columns, lon, own, strip, count):
    body = slice(OFF - 8, OFF + rows + 8)
    packed = strip_parts(lon, level, (rows + 16) // UNIT)
    first, last = 128 * columns[0], 128 * (columns[-1] + 1)
    got = moved(packed, strip[:, first:last], count)
    for i, (parts, side, table) in enumerate(zip(fields, sides, own)):
        mine = moved([p[body] for p in parts], table[...], count)
        side[body] = mine + got[:, 128 * i : 128 * i + 128]


def to_right(a):
    return pltpu.roll(a, 127, 1)


def to_left(a):
    return pltpu.roll(a, 1, 1)


def chunks(first, last, size):
    return [slice(r, r + size) for r in range(first, last, size)]


def around(rows):
    return chunks(OFF - 8, OFF + rows + 8, 24)


def moved_rows(here, by):
    return slice(here.start + by, here.stop + by)


def open_faces(rows, ocean, east, north):
    for here in around(rows):
        o = ocean[here]
        east[here] = 0.5 * (o * to_right(o))
        north[here] = 0.5 * (o * ocean[moved_rows(here, 1)])


def faces(a, b, mix, face):
    vel = a + b
    low = jnp.maximum(vel, 0.0) + mix
    return face * low, face * (low - vel)


def coefficients(rows, u, v, k, east, north, coef, above):
    for here in around(rows):
        up = moved_rows(here, 1)
        a, b = faces(v[here], v[up], k[here] + k[up], north[here])
        above[here] = a
        coef[3, here] = b
    for here in around(rows):
        below = moved_rows(here, -1)
        us, ks = u[here], k[here]
        a, b = faces(us, to_right(us), ks + to_right(ks), east[here])
        wa, wb = to_left(a), to_left(b)
        south = above[below]
        coef[0, here] = (1.0 - (a + wb)) - (above[here] + coef[3, below])
        coef[1, here] = b
        coef[2, here] = wa
        coef[4, here] = south


def stencil(c, q, here):
    mid = q[here]
    return (
        c[0] * mid
        + c[1] * to_right(mid)
        + c[2] * to_left(mid)
        + c[3] * q[moved_rows(here, 1)]
        + c[4] * q[moved_rows(here, -1)]
    )


def advance(rows, coef, side_coef, q, side):
    for step in range(STEPS):
        src, dst = step % 2, (step + 1) % 2
        last = step == STEPS - 1
        for here in chunks(OFF, OFF + rows, 32) if last else around(rows):
            c = [side_coef[i, here] for i in range(5)]
            side[dst, here] = stencil(c, side.at[src], here)
            c = [coef[i, here] for i in range(5)]
            for i in range(NTR):
                q[dst, i, here] = stencil(c, q.at[src, i], here)


def field_scratch(rows):
    ext = (rows + 32, 128)
    return [
        pltpu.VMEM((count,) + ext, jnp.float32)
        for count in (3, 3, 4, 2, 5, 5)
    ] + [
        pltpu.VMEM((2, NTR) + ext, jnp.float32),
        pltpu.VMEM((2,) + ext, jnp.float32),
    ]


def set_faces(x, levels, lat, lon, tables, scratch):
    rows = x.shape[1]
    own_q, own, strip, back = tables
    vel, side_vel, face = scratch[:3]
    ocean, side = vel.at[0], side_vel.at[0]
    unpack_field(ocean, FIELDS - 1, 0, levels, x, lat)
    side_arrays(rows, 0, [[ocean]], [side], [NTR], lon, [own], strip, 1)
    open_faces(rows, ocean, face.at[0], face.at[1])
    open_faces(rows, side, face.at[2], face.at[3])


def run_level(level, x, levels, lat, lon, tables, scratch, count):
    rows = x.shape[1]
    own_q, own, strip, back = tables
    vel, side_vel, face, above, coef, side_coef, q, side = scratch
    now = [q.at[0, i] for i in range(NTR)]
    three = [vel.at[i] for i in range(3)]
    for i, ref in enumerate(now + three):
        unpack_field(ref, i, level, levels, x, lat)
    side_arrays(
        rows,
        level,
        [now] + [[ref] for ref in three],
        [side.at[0]] + [side_vel.at[i] for i in range(3)],
        range(NTR),
        lon,
        [own_q, own, own, own],
        strip,
        count,
    )
    coefficients(rows, *three, face.at[0], face.at[1], coef, above.at[0])
    coefficients(
        rows, *(side_vel.at[i] for i in range(3)), face.at[2], face.at[3], side_coef, above.at[1]
    )
    advance(rows, coef, side_coef, q, side)
    body = slice(OFF, OFF + rows)
    ends = moved([side[0, body]], back[...], count)
    lane = lane_ids(rows)
    inner = (lane >= STEPS) & (lane < 128 - STEPS)
    return [
        jnp.where(inner, q[0, i, body], ends[:, 128 * i : 128 * i + 128]) for i in range(NTR)
    ]


def surface_kernel(order, accs, levels, slot, x, la, lb, wa, wb, *refs):
    tables, w_held, w_more, w_hbm = refs[:4], refs[4], refs[5], refs[6]
    out_q, out_send, out_keep = refs[7:10]
    scratch, surf, w_last, sem, sums = refs[10:18], refs[18], refs[19], refs[20], refs[21:]
    rows = x.shape[1]
    done_rows = w_held.shape[0] + w_more.shape[0]
    copy = pltpu.make_async_copy(w_hbm.at[pl.ds(done_rows, w_last.shape[0])], w_last, sem)
    copy.start()
    lat, lon = (la, lb), (wa, wb, 0)
    set_faces(x, levels, lat, lon, tables, scratch)
    ocean = x[field_index(FIELDS - 1, 0, levels)]
    for i, done in enumerate(run_level(0, x, levels, lat, lon, tables, scratch, 3)):
        out_q[i] = done
        surf[pl.ds(i, rows, stride=8), :] = done * ocean
    surf[pl.ds(NTR, rows, stride=8), :] = ocean
    for i in range(NTR + 1, 8):
        surf[pl.ds(i, rows, stride=8), :] = jnp.zeros((rows, 128), jnp.float32)
    for d in sums:
        d[...] = jnp.zeros_like(d)
    first = sub_ids(16) < 8
    kb = w_held.shape[1]

    def body(w, base, j, carry):
        i = j + base
        s = surf[pl.ds(pl.multiple_of(16 * i, 16), 16), :]
        lhs = jnp.concatenate(
            [jnp.where(first, s, 0.0), jnp.where(first, 0.0, s)], axis=1
        ).astype(jnp.bfloat16)
        for k in range(0, kb, 2):
            rhs = jnp.concatenate(
                [
                    jnp.concatenate([w[2 * j + r, k], w[2 * j + r, k + 1]], axis=1)
                    for r in range(2)
                ],
                axis=0,
            )
            part = jnp.dot(lhs, rhs, preferred_element_type=jnp.float32)
            for r in range(2):
                for kk in range(2):
                    d = sums[(k + kk) % accs]
                    at = pl.ds(
                        pl.multiple_of(8 * slot[k + kk, 2 * i + r], 8), 8
                    )
                    d[at, :] += part[8 * r : 8 * r + 8, 128 * kk : 128 * kk + 128]
        return carry

    start = 0
    for w in (w_held, w_more, w_last):
        if w is w_last:
            copy.wait()
        pairs = w.shape[0] // 2
        lax.fori_loop(0, pairs, functools.partial(body, w, start), 0, unroll=8)
        start += pairs
    chunk = ABD * (NTR + 1)
    half = len(order) // 2
    for place, owner in enumerate(order):
        ref, base = (out_keep, place) if place < half else (out_send, place - half)
        for f in range(NTR + 1):
            total = sums[0][pl.ds(owner * ABD * 8 + f, ABD, stride=8), :]
            for d in sums[1:]:
                total = total + d[pl.ds(owner * ABD * 8 + f, ABD, stride=8), :]
            at = base * chunk + f * ABD
            ref[at : at + ABD, :] = total


def surface(order, slot, tile, levels, lat, lon, tables, held, weights):
    rows = tile.shape[1]
    owners = len(order)
    accs = 2 if owners <= 32 else 1
    half = owners // 2 * ABD * (NTR + 1)
    last = (rows - sum(w.shape[0] for w in held),) + weights.shape[1:]
    return pl.pallas_call(
        functools.partial(surface_kernel, order, accs, levels),
        in_specs=[SCALARS] + [WHOLE] * 11 + [pl.BlockSpec(memory_space=pltpu.HBM)],
        out_specs=[WHOLE] * 3,
        scratch_shapes=field_scratch(rows)
        + [pltpu.VMEM((rows * 8 + 8, 128), jnp.float32)]
        + [pltpu.VMEM(last, weights.dtype), pltpu.SemaphoreType.DMA]
        + [pltpu.VMEM((owners * ABD * 8 + 8, 128), jnp.float32)] * accs,
        out_shape=[
            jax.ShapeDtypeStruct((NTR, rows, 128), jnp.float32),
            jax.ShapeDtypeStruct((half, 128), jnp.float32),
            jax.ShapeDtypeStruct((half, 128), jnp.float32),
        ],
        compiler_params=pltpu.CompilerParams(vmem_limit_bytes=24 << 20),
        cost_estimate=took(7),
        name="surface",
    )(slot, in_vmem(tile), *lat, *lon, *tables, *(in_vmem(w) for w in held), in_hbm(weights))


def deep_kernel(first, levels, x, la, lb, oa, ob, wa, wb, *refs):
    tables, base, out, scratch = refs[:4], refs[4], refs[5], refs[6:]
    lat = (la, lb)
    level = pl.program_id(0) + first

    @pl.when(pl.program_id(0) == 0)
    def _():
        set_faces(x, levels, lat, (oa, ob, 0), tables, scratch)

    if first == 0:
        @pl.when(level == 0)
        def _():
            out[:, 0] = base[...]

    @pl.when(level > 0)
    def _():
        lon = (wa, wb, 1)
        for i, done in enumerate(run_level(level, x, levels, lat, lon, tables, scratch, COUNT)):
            out[i, 0] = done


def deep(tile, levels, lat, lon0, lon, tables, base, first, count):
    rows = tile.shape[1]
    return pl.pallas_call(
        functools.partial(deep_kernel, first, levels),
        grid=(count,),
        in_specs=[WHOLE] * 11 + [pl.BlockSpec(memory_space=pl.ANY) if first else WHOLE],
        out_specs=pl.BlockSpec((NTR, 1, rows, 128), lambda l: (0, l + first, 0, 0)),
        out_shape=jax.ShapeDtypeStruct((NTR, levels, rows, 128), jnp.float32),
        scratch_shapes=field_scratch(rows),
        input_output_aliases={11: 0} if first else {},
        compiler_params=pltpu.CompilerParams(vmem_limit_bytes=16 << 20),
        cost_estimate=took(1.3 * count),
        name="deep",
    )(in_vmem(tile), *lat, *lon0, *lon, *tables, base)


def swap(first, second, axis, ring):
    n = lax.axis_size(axis)
    even = [(i, i + 1) for i in range(0, n - 1, 2)]
    odd = [(i, (i + 1) % n) for i in range(1, n if ring else n - 1, 2)]
    second = lax.ppermute(second, axis, odd + [(j, i) for i, j in odd])
    first = lax.ppermute(first, axis, even + [(j, i) for i, j in even])
    return first, second


def partner(a, mask, n):
    return lax.ppermute(a, AXES, [(i, i ^ mask) for i in range(n)])


def rounds_of(owners):
    bits = owners.bit_length() - 1
    out, at = [(0, 1)], 1
    while at < bits:
        width = min(2, bits - at)
        out.append((at, width))
        at += width
    return out


def cuts(levels, rounds):
    between = [2 + (levels - 4) * i // (rounds - 2) for i in range(rounds - 1)]
    return [0] + between + [levels]


def order_of(owners):
    def key(owner):
        return tuple((-(owner >> at)) & ((1 << width) - 1) for at, width in rounds_of(owners))
    return sorted(range(owners), key=key)


def per_device(tracers, velocity, mixing, land_mask, remap_weights, remap_dest):
    owners = lax.axis_size("gx") * lax.axis_size("gy")
    levels = tracers.shape[1]
    me = lax.axis_index("gx") * lax.axis_size("gy") + lax.axis_index("gy")
    dest = remap_dest[:, 0].T
    slot = jnp.bitwise_xor(dest // ABD, me) * ABD + dest % ABD

    arrays = (tracers, velocity, mixing, land_mask)
    strips = lat_pack(*arrays)
    lat = swap(*strips, "gy", False)
    slot, first = lax.optimization_barrier((slot, strips[0]))
    tile, held = fetch(slot, arrays, remap_weights)
    lat, tile, held = lax.optimization_barrier((lat, tile, held))
    first, second = lon_pack(lat, tile, levels)
    lon0 = swap(first, second, "gx", True)
    lat, first = lax.optimization_barrier((lat, first))
    first, second, more, *tables = lon_pack(lat, tile, levels, remap_weights)
    lon0, first, more, tables = lax.optimization_barrier((lon0, first, more, tables))
    lon = swap(first, second, "gx", True)

    order = order_of(owners)
    done, send, keep = surface(
        order, slot, tile, levels, lat, lon0, tables, (held, more), remap_weights
    )
    lon, send = lax.optimization_barrier((lon, send))
    rounds = rounds_of(owners)
    cut = cuts(levels, len(rounds))
    parts = [keep, send]
    values = done
    for i, (at, width) in enumerate(rounds):
        got = [partner(parts[j], (-j % (1 << width)) << at, owners) for j in range(1, 1 << width)]
        values = deep(tile, levels, lat, lon0, lon, tables, values, cut[i], cut[i + 1] - cut[i])
        got, values = lax.optimization_barrier((got, values))
        total = parts[0]
        for g in got:
            total = total + g
        if i < len(rounds) - 1:
            lon, total = lax.optimization_barrier((lon, total))
            parts = total.reshape((1 << rounds[i + 1][1], -1, 128))
    atmo = total.reshape(NTR + 1, ABD, 128).transpose(1, 0, 2)
    return values, atmo


def solution(mesh):
    placed = (
        P(None, None, "gy", "gx"),
        P(None, None, "gy", "gx"),
        P(None, "gy", "gx"),
        P("gy", "gx"),
        P("gy", None, "gx", None),
        P("gy", "gx", None),
    )
    return jax.shard_map(
        per_device,
        mesh=mesh,
        in_specs=placed,
        out_specs=(P(None, None, "gy", "gx"), P(("gx", "gy"), None, None)),
        check_vma=False,
    )
```

```python
import functools

import jax
import jax.numpy as jnp
from jax import lax
from jax.experimental import pallas as pl
from jax.experimental.pallas import tpu as pltpu
from jax.sharding import PartitionSpec as P

STEPS = 4
ABD = 16
NTR = 4
FIELDS = 8
OFF = 16
FIRST, SECOND = 3, 3
COUNT = 2
UNIT = 16
AXES = ("gx", "gy")


WHOLE = pl.BlockSpec(memory_space=pltpu.VMEM)
SCALARS = pl.BlockSpec(memory_space=pltpu.SMEM)


def took(us):
    return pl.CostEstimate(flops=0, bytes_accessed=int(us * 3.5e6), transcendentals=0)


def in_hbm(a):
    return pltpu.with_memory_space_constraint(a, pltpu.HBM)


def in_vmem(a):
    return pltpu.with_memory_space_constraint(a, pltpu.VMEM)


def lane_ids(rows):
    return lax.broadcasted_iota(jnp.int32, (rows, 128), 1)


def sub_ids(rows):
    return lax.broadcasted_iota(jnp.int32, (rows, 128), 0)


def parity(axis):
    return lax.axis_index(axis) & 1


def pick(odd, a, b):
    return jnp.where(odd == 0, a, b), jnp.where(odd == 0, b, a)


def lat_pack_kernel(tl, vl, ml, ol, th, vh, mh, oh, first_ref, second_ref):
    top = sub_ids(8) < 4
    for level in range(tl.shape[1]):

        def fields(t, v, m, o):
            out = [t[i, level] for i in range(NTR)] + [v[0, level], v[1, level], m[level]]
            out.append(o[...].astype(jnp.float32) if level == 0 else m[level])
            return out

        low, high = fields(tl, vl, ml, ol), fields(th, vh, mh, oh)
        for p in range(FIELDS // 2):
            here = slice(8 * p, 8 * p + 8)
            a, b = low[2 * p], low[2 * p + 1]
            south = jnp.where(top, a, pltpu.roll(b, 4, 0))
            a, b = high[2 * p], high[2 * p + 1]
            north = jnp.where(top, pltpu.roll(a, 4, 0), b)
            first_ref[level, here], second_ref[level, here] = pick(parity("gy"), north, south)


def lat_pack(tracers, velocity, mixing, ocean):
    levels, rows = tracers.shape[1:3]
    last = rows // 8 - 1

    def specs(block):
        return [
            pl.BlockSpec((NTR, levels, 8, 128), lambda l: (0, 0, block, 0)),
            pl.BlockSpec((2, levels, 8, 128), lambda l: (0, 0, block, 0)),
            pl.BlockSpec((levels, 8, 128), lambda l: (0, block, 0)),
            pl.BlockSpec((8, 128), lambda l: (block, 0)),
        ]

    arrays = [in_hbm(a) for a in (tracers, velocity, mixing, ocean)]
    strip = jax.ShapeDtypeStruct((levels, 32, 128), jnp.float32)
    return pl.pallas_call(
        lat_pack_kernel,
        grid=(1,),
        in_specs=specs(0) + specs(last),
        out_specs=[WHOLE] * 2,
        out_shape=[strip, strip],
        compiler_params=pltpu.CompilerParams(vmem_limit_bytes=4 << 20),
        cost_estimate=took(2),
        name="lat_pack",
    )(*arrays, *arrays)


def field_index(f, level, levels):
    return (FIELDS - 1) * levels if f == FIELDS - 1 else f * levels + level


def tile_copies(levels, t, v, m, o, out, mask, sems):
    sources = [t.at[i] for i in range(NTR)] + [v.at[0], v.at[1], m]
    copies = [pltpu.make_async_copy(o, mask, sems.at[FIELDS - 1])]
    for f, source in enumerate(sources):
        target = out.at[pl.ds(f * levels, levels)]
        copies.append(pltpu.make_async_copy(source.at[pl.ds(0, levels)], target, sems.at[f]))
    return copies


def tile_shape(levels, rows):
    return ((FIELDS - 1) * levels + 1, rows, 128)


def finish_tile(copies, out, mask):
    for copy in copies:
        copy.wait()
    out[out.shape[0] - 1] = mask[...].astype(jnp.float32)


def lat_halo_blocks(lat, f, level):
    first, second = lat
    p, odd = f // 2, f % 2
    here = slice(8 * p, 8 * p + 8)
    n, s = pick(parity("gy"), first[level, here], second[level, here])
    if odd:
        return s, pltpu.roll(n, 4, 0)
    return pltpu.roll(s, 4, 0), n


def one_hot(ref, rows, cols, match):
    i, j = sub_ids(128), lane_ids(128)
    for r in range(0, rows, 128):
        for c in range(0, cols, 128):
            hit = match(i, j, r // 128, c // 128)
            ref[r : r + 128, c : c + 128] = jnp.where(hit, 1.0, 0.0).astype(jnp.bfloat16)


def own_match(i, j):
    s = j & 31
    return ((s < 8) & (i == s + 120)) | ((s >= 16) & (s < 24) & (i == s - 16))


def strip_match(i, j, f):
    s = j & 31
    west = (s >= 12) & (s < 16) & (i == 4 * f + s - 12)
    east = (s >= 8) & (s < 12) & (i == 4 * f + 4 + s - 8)
    return west | east


def tables_kernel(own_q, own, strip, back):
    one_hot(own_q, NTR * 128, 128, lambda i, j, r, c: own_match(i, j) & ((j >> 5) == r))
    one_hot(own, 128, 128, lambda i, j, r, c: own_match(i, j))

    def strips(i, j, odd, c):
        if c > 0:
            f = NTR + c - 1
            if f % 2 != odd:
                return i < 0
            return strip_match(i, j, f)
        hit = i < 0
        for f in range(odd, NTR, 2):
            hit |= strip_match(i, j, f) & ((j >> 5) == f)
        return hit

    one_hot(strip, strip.shape[0], strip.shape[1], strips)
    one_hot(
        back,
        128,
        NTR * 128,
        lambda i, j, r, c: (i == 32 * c + 16 + j) & (j < 4)
        | (i == 32 * c + 4 + j - 124) & (j >= 124),
    )


TABLES = [(NTR * 128, 128), (128, 128), (256, 5 * 128), (128, NTR * 128)]


def unit_place(n):
    return UNIT * (n // 4), 32 * (n % 4)


def strip_rows(count, rows):
    return UNIT * ((count * ((rows + 16) // UNIT) + 3) // 4)


def pack_columns(first, levels, x, lat, first_ref, second_ref, count):
    units = (x.shape[1] + 16) // UNIT
    lane = lane_ids(UNIT)
    west = east = jnp.zeros((UNIT, 128), jnp.float32)
    for l in range(count):
        level = first + l
        fields = range(FIELDS if level == 0 else FIELDS - 1)
        whole = []
        for f in fields:
            s, n = lat_halo_blocks(lat, f, level)
            whole.append(jnp.concatenate([s, x[field_index(f, level, levels)], n], axis=0))
        for r in range(units):
            place, base = unit_place(l * units + r)
            for f in fields:
                at = base + 4 * f
                turned = pltpu.roll(whole[f][UNIT * r : UNIT * r + UNIT], (at - 124) % 128, 1)
                east = jnp.where((lane >= at) & (lane < at + 4), turned, east)
                to = (at + 4) % 128
                west = jnp.where((lane >= to) & (lane < to + 4), turned, west)
            if base == 96 or (l == count - 1 and r == units - 1):
                here = slice(place, place + UNIT)
                first_ref[here], second_ref[here] = pick(parity("gx"), east, west)
                west = east = jnp.zeros((UNIT, 128), jnp.float32)


def fetch_kernel(after, t, v, m, o, w, x, out, mask, sems, sem):
    copies = tile_copies(t.shape[1], t, v, m, o, x, mask, sems)
    copies.append(pltpu.make_async_copy(w.at[pl.ds(0, out.shape[0])], out, sem))
    for copy in copies:
        copy.start()
    finish_tile(copies[:-1], x, mask)
    copies[-1].wait()


def fetch(after, arrays, weights):
    levels, rows = arrays[0].shape[1:3]
    part = (rows * FIRST // 8,) + weights.shape[1:]
    return pl.pallas_call(
        fetch_kernel,
        in_specs=[pl.BlockSpec(memory_space=pl.ANY)]
        + [pl.BlockSpec(memory_space=pltpu.HBM)] * 5,
        out_specs=[WHOLE] * 2,
        out_shape=[
            pltpu.VMEM(tile_shape(levels, rows), jnp.float32),
            pltpu.VMEM(part, weights.dtype),
        ],
        scratch_shapes=[
            pltpu.VMEM(arrays[3].shape, jnp.int32),
            pltpu.SemaphoreType.DMA((FIELDS,)),
            pltpu.SemaphoreType.DMA,
        ],
        compiler_params=pltpu.CompilerParams(vmem_limit_bytes=2 << 20),
        cost_estimate=took(3),
        name="fetch",
    )(after, *(in_hbm(a) for a in (*arrays, weights)))


def lon_pack_kernel(levels, la, lb, x, first_ref, second_ref):
    pack_columns(0, levels, x, (la, lb), first_ref, second_ref, 1)


def others_pack_kernel(levels, skip, la, lb, x, w, first_ref, second_ref, *refs):
    out, own_q, own, strip, back, sem = refs
    copy = pltpu.make_async_copy(w.at[pl.ds(skip, out.shape[0])], out, sem)
    copy.start()
    pack_columns(1, levels, x, (la, lb), first_ref, second_ref, levels - 1)
    tables_kernel(own_q, own, strip, back)
    copy.wait()


def lon_pack(lat, tile, levels, weights=None):
    rows = tile.shape[1]
    count = levels - 1 if weights is not None else 1
    out = [jax.ShapeDtypeStruct((strip_rows(count, rows), 128), jnp.float32)] * 2
    if weights is None:
        kernel = functools.partial(lon_pack_kernel, levels)
    else:
        kernel = functools.partial(others_pack_kernel, levels, rows * FIRST // 8)
        out.append(pltpu.VMEM((rows * SECOND // 8,) + weights.shape[1:], weights.dtype))
        out += [pltpu.VMEM(shape, jnp.bfloat16) for shape in TABLES]
    more = [] if weights is None else [in_hbm(weights)]
    return pl.pallas_call(
        kernel,
        in_specs=[WHOLE] * 3 + [pl.BlockSpec(memory_space=pltpu.HBM)] * len(more),
        out_specs=[WHOLE] * len(out),
        out_shape=out,
        scratch_shapes=[pltpu.SemaphoreType.DMA] * len(more),
        compiler_params=pltpu.CompilerParams(vmem_limit_bytes=4 << 20),
        cost_estimate=took(0.3 if weights is None else 2),
        name="lon_pack",
    )(*lat, in_vmem(tile), *more)


def unpack_field(ext, f, level, levels, x, lat):
    rows = x.shape[1]
    s, n = lat_halo_blocks(lat, f, level)
    ext[OFF - 8 : OFF] = s
    ext[OFF : OFF + rows] = x[field_index(f, level, levels)]
    ext[OFF + rows : OFF + rows + 8] = n


def terms(x, count):
    out = []
    for i in range(count):
        out.append(x.astype(jnp.bfloat16))
        if i < count - 1:
            x = x - out[-1].astype(jnp.float32)
    return out


def moved(parts, table, count):
    n = parts[0].shape[0]
    split = [terms(p, count) for p in parts]
    lhs = jnp.concatenate(
        [jnp.concatenate([p[i] for p in split], axis=1) for i in range(count)], axis=0
    )
    out = jnp.dot(lhs, table, preferred_element_type=jnp.float32)
    total = out[:n]
    for i in range(1, count):
        total = total + out[i * n : i * n + n]
    return total


def strip_parts(lon, level, units):
    near = lane_ids(UNIT) % 8 < 4
    first, second, base = lon
    even, odd = [], []
    for r in range(units):
        row, lane = level_unit(level - base, r, units)
        here = pl.ds(row, UNIT)
        e, w = pick(parity("gx"), first[here, :], second[here, :])
        even.append(pltpu.roll(jnp.where(near, w, e), (128 - lane) & 127, 1))
        odd.append(pltpu.roll(jnp.where(near, e, w), (128 - lane) & 127, 1))
    return [jnp.concatenate(even, axis=0), jnp.concatenate(odd, axis=0)]


def level_unit(l, r, units):
    n = l * units + r
    if isinstance(n, int):
        return unit_place(n)
    return pl.multiple_of(UNIT * (n >> 2), UNIT), 32 * (n & 3)


def side_arrays(rows, level, fields, sides, columns, lon, own, strip, count):
    body = slice(OFF - 8, OFF + rows + 8)
    packed = strip_parts(lon, level, (rows + 16) // UNIT)
    first, last = 128 * columns[0], 128 * (columns[-1] + 1)
    got = moved(packed, strip[:, first:last], count)
    for i, (parts, side, table) in enumerate(zip(fields, sides, own)):
        mine = moved([p[body] for p in parts], table[...], count)
        side[body] = mine + got[:, 128 * i : 128 * i + 128]


def to_right(a):
    return pltpu.roll(a, 127, 1)


def to_left(a):
    return pltpu.roll(a, 1, 1)


def chunks(first, last, size):
    return [slice(r, r + size) for r in range(first, last, size)]


def around(rows):
    return chunks(OFF - 8, OFF + rows + 8, 24)


def moved_rows(here, by):
    return slice(here.start + by, here.stop + by)


def open_faces(rows, ocean, east, north):
    for here in around(rows):
        o = ocean[here]
        east[here] = 0.5 * (o * to_right(o))
        north[here] = 0.5 * (o * ocean[moved_rows(here, 1)])


def faces(a, b, mix, face):
    vel = a + b
    low = jnp.maximum(vel, 0.0) + mix
    return face * low, face * (low - vel)


def coefficients(rows, u, v, k, east, north, coef, above):
    for here in around(rows):
        up = moved_rows(here, 1)
        a, b = faces(v[here], v[up], k[here] + k[up], north[here])
        above[here] = a
        coef[3, here] = b
    for here in around(rows):
        below = moved_rows(here, -1)
        us, ks = u[here], k[here]
        a, b = faces(us, to_right(us), ks + to_right(ks), east[here])
        wa, wb = to_left(a), to_left(b)
        south = above[below]
        coef[0, here] = (1.0 - (a + wb)) - (above[here] + coef[3, below])
        coef[1, here] = b
        coef[2, here] = wa
        coef[4, here] = south


def stencil(c, q, here):
    mid = q[here]
    return (
        c[0] * mid
        + c[1] * to_right(mid)
        + c[2] * to_left(mid)
        + c[3] * q[moved_rows(here, 1)]
        + c[4] * q[moved_rows(here, -1)]
    )


def advance(rows, coef, side_coef, q, side):
    for step in range(STEPS):
        src, dst = step % 2, (step + 1) % 2
        last = step == STEPS - 1
        for here in chunks(OFF, OFF + rows, 32) if last else around(rows):
            c = [side_coef[i, here] for i in range(5)]
            side[dst, here] = stencil(c, side.at[src], here)
            c = [coef[i, here] for i in range(5)]
            for i in range(NTR):
                q[dst, i, here] = stencil(c, q.at[src, i], here)


def field_scratch(rows):
    ext = (rows + 32, 128)
    return [
        pltpu.VMEM((count,) + ext, jnp.float32)
        for count in (3, 3, 4, 2, 5, 5)
    ] + [
        pltpu.VMEM((2, NTR) + ext, jnp.float32),
        pltpu.VMEM((2,) + ext, jnp.float32),
    ]


def set_faces(x, levels, lat, lon, tables, scratch):
    rows = x.shape[1]
    own_q, own, strip, back = tables
    vel, side_vel, face = scratch[:3]
    ocean, side = vel.at[0], side_vel.at[0]
    unpack_field(ocean, FIELDS - 1, 0, levels, x, lat)
    side_arrays(rows, 0, [[ocean]], [side], [NTR], lon, [own], strip, 1)
    open_faces(rows, ocean, face.at[0], face.at[1])
    open_faces(rows, side, face.at[2], face.at[3])


def run_level(level, x, levels, lat, lon, tables, scratch, count):
    rows = x.shape[1]
    own_q, own, strip, back = tables
    vel, side_vel, face, above, coef, side_coef, q, side = scratch
    now = [q.at[0, i] for i in range(NTR)]
    three = [vel.at[i] for i in range(3)]
    for i, ref in enumerate(now + three):
        unpack_field(ref, i, level, levels, x, lat)
    side_arrays(
        rows,
        level,
        [now] + [[ref] for ref in three],
        [side.at[0]] + [side_vel.at[i] for i in range(3)],
        range(NTR),
        lon,
        [own_q, own, own, own],
        strip,
        count,
    )
    coefficients(rows, *three, face.at[0], face.at[1], coef, above.at[0])
    coefficients(
        rows, *(side_vel.at[i] for i in range(3)), face.at[2], face.at[3], side_coef, above.at[1]
    )
    advance(rows, coef, side_coef, q, side)
    body = slice(OFF, OFF + rows)
    ends = moved([side[0, body]], back[...], count)
    lane = lane_ids(rows)
    inner = (lane >= STEPS) & (lane < 128 - STEPS)
    return [
        jnp.where(inner, q[0, i, body], ends[:, 128 * i : 128 * i + 128]) for i in range(NTR)
    ]


def surface_kernel(order, accs, levels, slot, x, la, lb, wa, wb, *refs):
    tables, w_held, w_more, w_hbm = refs[:4], refs[4], refs[5], refs[6]
    out_q, out_send, out_keep = refs[7:10]
    scratch, surf, w_last, sem, sums = refs[10:18], refs[18], refs[19], refs[20], refs[21:]
    rows = x.shape[1]
    done_rows = w_held.shape[0] + w_more.shape[0]
    copy = pltpu.make_async_copy(w_hbm.at[pl.ds(done_rows, w_last.shape[0])], w_last, sem)
    copy.start()
    lat, lon = (la, lb), (wa, wb, 0)
    set_faces(x, levels, lat, lon, tables, scratch)
    ocean = x[field_index(FIELDS - 1, 0, levels)]
    for i, done in enumerate(run_level(0, x, levels, lat, lon, tables, scratch, 2)):
        out_q[i] = done
        surf[pl.ds(i, rows, stride=8), :] = done * ocean
    surf[pl.ds(NTR, rows, stride=8), :] = ocean
    for i in range(NTR + 1, 8):
        surf[pl.ds(i, rows, stride=8), :] = jnp.zeros((rows, 128), jnp.float32)
    for d in sums:
        d[...] = jnp.zeros_like(d)
    first = sub_ids(16) < 8
    kb = w_held.shape[1]

    def body(w, base, j, carry):
        i = j + base
        s = surf[pl.ds(pl.multiple_of(16 * i, 16), 16), :]
        lhs = jnp.concatenate(
            [jnp.where(first, s, 0.0), jnp.where(first, 0.0, s)], axis=1
        ).astype(jnp.bfloat16)
        for k in range(0, kb, 2):
            rhs = jnp.concatenate(
                [
                    jnp.concatenate([w[2 * j + r, k], w[2 * j + r, k + 1]], axis=1)
                    for r in range(2)
                ],
                axis=0,
            )
            part = jnp.dot(lhs, rhs, preferred_element_type=jnp.float32)
            for r in range(2):
                for kk in range(2):
                    d = sums[(k + kk) % accs]
                    at = pl.ds(
                        pl.multiple_of(8 * slot[k + kk, 2 * i + r], 8), 8
                    )
                    d[at, :] += part[8 * r : 8 * r + 8, 128 * kk : 128 * kk + 128]
        return carry

    start = 0
    for w in (w_held, w_more, w_last):
        if w is w_last:
            copy.wait()
        pairs = w.shape[0] // 2
        lax.fori_loop(0, pairs, functools.partial(body, w, start), 0, unroll=8)
        start += pairs
    chunk = ABD * (NTR + 1)
    half = len(order) // 2
    for place, owner in enumerate(order):
        ref, base = (out_keep, place) if place < half else (out_send, place - half)
        for f in range(NTR + 1):
            total = sums[0][pl.ds(owner * ABD * 8 + f, ABD, stride=8), :]
            for d in sums[1:]:
                total = total + d[pl.ds(owner * ABD * 8 + f, ABD, stride=8), :]
            at = base * chunk + f * ABD
            ref[at : at + ABD, :] = total


def surface(order, slot, tile, levels, lat, lon, tables, held, weights):
    rows = tile.shape[1]
    owners = len(order)
    accs = 2 if owners <= 32 else 1
    half = owners // 2 * ABD * (NTR + 1)
    last = (rows - sum(w.shape[0] for w in held),) + weights.shape[1:]
    return pl.pallas_call(
        functools.partial(surface_kernel, order, accs, levels),
        in_specs=[SCALARS] + [WHOLE] * 11 + [pl.BlockSpec(memory_space=pltpu.HBM)],
        out_specs=[WHOLE] * 3,
        scratch_shapes=field_scratch(rows)
        + [pltpu.VMEM((rows * 8 + 8, 128), jnp.float32)]
        + [pltpu.VMEM(last, weights.dtype), pltpu.SemaphoreType.DMA]
        + [pltpu.VMEM((owners * ABD * 8 + 8, 128), jnp.float32)] * accs,
        out_shape=[
            jax.ShapeDtypeStruct((NTR, rows, 128), jnp.float32),
            jax.ShapeDtypeStruct((half, 128), jnp.float32),
            jax.ShapeDtypeStruct((half, 128), jnp.float32),
        ],
        compiler_params=pltpu.CompilerParams(vmem_limit_bytes=24 << 20),
        cost_estimate=took(7),
        name="surface",
    )(slot, in_vmem(tile), *lat, *lon, *tables, *(in_vmem(w) for w in held), in_hbm(weights))


def deep_kernel(first, levels, x, la, lb, oa, ob, wa, wb, *refs):
    tables, base, out, scratch = refs[:4], refs[4], refs[5], refs[6:]
    lat = (la, lb)
    level = pl.program_id(0) + first

    @pl.when(pl.program_id(0) == 0)
    def _():
        set_faces(x, levels, lat, (oa, ob, 0), tables, scratch)

    if first == 0:
        @pl.when(level == 0)
        def _():
            out[:, 0] = base[...]

    @pl.when(level > 0)
    def _():
        lon = (wa, wb, 1)
        for i, done in enumerate(run_level(level, x, levels, lat, lon, tables, scratch, COUNT)):
            out[i, 0] = done


def deep(tile, levels, lat, lon0, lon, tables, base, first, count):
    rows = tile.shape[1]
    return pl.pallas_call(
        functools.partial(deep_kernel, first, levels),
        grid=(count,),
        in_specs=[WHOLE] * 11 + [pl.BlockSpec(memory_space=pl.ANY) if first else WHOLE],
        out_specs=pl.BlockSpec((NTR, 1, rows, 128), lambda l: (0, l + first, 0, 0)),
        out_shape=jax.ShapeDtypeStruct((NTR, levels, rows, 128), jnp.float32),
        scratch_shapes=field_scratch(rows),
        input_output_aliases={11: 0} if first else {},
        compiler_params=pltpu.CompilerParams(vmem_limit_bytes=16 << 20),
        cost_estimate=took(1.3 * count),
        name="deep",
    )(in_vmem(tile), *lat, *lon0, *lon, *tables, base)


def swap(first, second, axis, ring):
    n = lax.axis_size(axis)
    even = [(i, i + 1) for i in range(0, n - 1, 2)]
    odd = [(i, (i + 1) % n) for i in range(1, n if ring else n - 1, 2)]
    second = lax.ppermute(second, axis, odd + [(j, i) for i, j in odd])
    first = lax.ppermute(first, axis, even + [(j, i) for i, j in even])
    return first, second


def partner(a, mask, n):
    return lax.ppermute(a, AXES, [(i, i ^ mask) for i in range(n)])


def rounds_of(owners):
    bits = owners.bit_length() - 1
    out, at = [(0, 1)], 1
    while at < bits:
        width = min(2, bits - at)
        out.append((at, width))
        at += width
    return out


def cuts(levels, rounds):
    between = [2 + (levels - 4) * i // (rounds - 2) for i in range(rounds - 1)]
    return [0] + between + [levels]


def order_of(owners):
    def key(owner):
        return tuple((-(owner >> at)) & ((1 << width) - 1) for at, width in rounds_of(owners))
    return sorted(range(owners), key=key)


def per_device(tracers, velocity, mixing, land_mask, remap_weights, remap_dest):
    owners = lax.axis_size("gx") * lax.axis_size("gy")
    levels = tracers.shape[1]
    me = lax.axis_index("gx") * lax.axis_size("gy") + lax.axis_index("gy")
    dest = remap_dest[:, 0].T
    slot = jnp.bitwise_xor(dest // ABD, me) * ABD + dest % ABD

    arrays = (tracers, velocity, mixing, land_mask)
    strips = lat_pack(*arrays)
    lat = swap(*strips, "gy", False)
    slot, first = lax.optimization_barrier((slot, strips[0]))
    tile, held = fetch(slot, arrays, remap_weights)
    lat, tile, held = lax.optimization_barrier((lat, tile, held))
    first, second = lon_pack(lat, tile, levels)
    lon0 = swap(first, second, "gx", True)
    lat, first = lax.optimization_barrier((lat, first))
    first, second, more, *tables = lon_pack(lat, tile, levels, remap_weights)
    lon0, first, more, tables = lax.optimization_barrier((lon0, first, more, tables))
    lon = swap(first, second, "gx", True)

    order = order_of(owners)
    done, send, keep = surface(
        order, slot, tile, levels, lat, lon0, tables, (held, more), remap_weights
    )
    lon, send = lax.optimization_barrier((lon, send))
    rounds = rounds_of(owners)
    cut = cuts(levels, len(rounds))
    parts = [keep, send]
    values = done
    for i, (at, width) in enumerate(rounds):
        got = [partner(parts[j], (-j % (1 << width)) << at, owners) for j in range(1, 1 << width)]
        values = deep(tile, levels, lat, lon0, lon, tables, values, cut[i], cut[i + 1] - cut[i])
        got, values = lax.optimization_barrier((got, values))
        total = parts[0]
        for g in got:
            total = total + g
        if i < len(rounds) - 1:
            lon, total = lax.optimization_barrier((lon, total))
            parts = total.reshape((1 << rounds[i + 1][1], -1, 128))
    atmo = total.reshape(NTR + 1, ABD, 128).transpose(1, 0, 2)
    return values, atmo


def solution(mesh):
    placed = (
        P(None, None, "gy", "gx"),
        P(None, None, "gy", "gx"),
        P(None, "gy", "gx"),
        P("gy", "gx"),
        P("gy", None, "gx", None),
        P("gy", "gx", None),
    )
    return jax.shard_map(
        per_device,
        mesh=mesh,
        in_specs=placed,
        out_specs=(P(None, None, "gy", "gx"), P(("gx", "gy"), None, None)),
        check_vma=False,
    )
```

```python
import functools

import jax
import jax.numpy as jnp
from jax import lax
from jax.experimental import pallas as pl
from jax.experimental.pallas import tpu as pltpu
from jax.sharding import PartitionSpec as P

STEPS = 4
ABD = 16
NTR = 4
FIELDS = 8
OFF = 16
FIRST, SECOND = 4, 2
COUNT = 2
UNIT = 16
AXES = ("gx", "gy")


WHOLE = pl.BlockSpec(memory_space=pltpu.VMEM)
SCALARS = pl.BlockSpec(memory_space=pltpu.SMEM)


def took(us):
    return pl.CostEstimate(flops=0, bytes_accessed=int(us * 3.5e6), transcendentals=0)


def in_hbm(a):
    return pltpu.with_memory_space_constraint(a, pltpu.HBM)


def in_vmem(a):
    return pltpu.with_memory_space_constraint(a, pltpu.VMEM)


def lane_ids(rows):
    return lax.broadcasted_iota(jnp.int32, (rows, 128), 1)


def sub_ids(rows):
    return lax.broadcasted_iota(jnp.int32, (rows, 128), 0)


def parity(axis):
    return lax.axis_index(axis) & 1


def pick(odd, a, b):
    return jnp.where(odd == 0, a, b), jnp.where(odd == 0, b, a)


def lat_pack_kernel(tl, vl, ml, ol, th, vh, mh, oh, first_ref, second_ref):
    top = sub_ids(8) < 4
    for level in range(tl.shape[1]):

        def fields(t, v, m, o):
            out = [t[i, level] for i in range(NTR)] + [v[0, level], v[1, level], m[level]]
            out.append(o[...].astype(jnp.float32) if level == 0 else m[level])
            return out

        low, high = fields(tl, vl, ml, ol), fields(th, vh, mh, oh)
        for p in range(FIELDS // 2):
            here = slice(8 * p, 8 * p + 8)
            a, b = low[2 * p], low[2 * p + 1]
            south = jnp.where(top, a, pltpu.roll(b, 4, 0))
            a, b = high[2 * p], high[2 * p + 1]
            north = jnp.where(top, pltpu.roll(a, 4, 0), b)
            first_ref[level, here], second_ref[level, here] = pick(parity("gy"), north, south)


def lat_pack(tracers, velocity, mixing, ocean):
    levels, rows = tracers.shape[1:3]
    last = rows // 8 - 1

    def specs(block):
        return [
            pl.BlockSpec((NTR, levels, 8, 128), lambda l: (0, 0, block, 0)),
            pl.BlockSpec((2, levels, 8, 128), lambda l: (0, 0, block, 0)),
            pl.BlockSpec((levels, 8, 128), lambda l: (0, block, 0)),
            pl.BlockSpec((8, 128), lambda l: (block, 0)),
        ]

    arrays = [in_hbm(a) for a in (tracers, velocity, mixing, ocean)]
    strip = jax.ShapeDtypeStruct((levels, 32, 128), jnp.float32)
    return pl.pallas_call(
        lat_pack_kernel,
        grid=(1,),
        in_specs=specs(0) + specs(last),
        out_specs=[WHOLE] * 2,
        out_shape=[strip, strip],
        compiler_params=pltpu.CompilerParams(vmem_limit_bytes=4 << 20),
        cost_estimate=took(2),
        name="lat_pack",
    )(*arrays, *arrays)


def field_index(f, level, levels):
    return (FIELDS - 1) * levels if f == FIELDS - 1 else f * levels + level


def tile_copies(levels, t, v, m, o, out, mask, sems):
    sources = [t.at[i] for i in range(NTR)] + [v.at[0], v.at[1], m]
    copies = [pltpu.make_async_copy(o, mask, sems.at[FIELDS - 1])]
    for f, source in enumerate(sources):
        target = out.at[pl.ds(f * levels, levels)]
        copies.append(pltpu.make_async_copy(source.at[pl.ds(0, levels)], target, sems.at[f]))
    return copies


def tile_shape(levels, rows):
    return ((FIELDS - 1) * levels + 1, rows, 128)


def finish_tile(copies, out, mask):
    for copy in copies:
        copy.wait()
    out[out.shape[0] - 1] = mask[...].astype(jnp.float32)


def lat_halo_blocks(lat, f, level):
    first, second = lat
    p, odd = f // 2, f % 2
    here = slice(8 * p, 8 * p + 8)
    n, s = pick(parity("gy"), first[level, here], second[level, here])
    if odd:
        return s, pltpu.roll(n, 4, 0)
    return pltpu.roll(s, 4, 0), n


def one_hot(ref, rows, cols, match):
    i, j = sub_ids(128), lane_ids(128)
    for r in range(0, rows, 128):
        for c in range(0, cols, 128):
            hit = match(i, j, r // 128, c // 128)
            ref[r : r + 128, c : c + 128] = jnp.where(hit, 1.0, 0.0).astype(jnp.bfloat16)


def own_match(i, j):
    s = j & 31
    return ((s < 8) & (i == s + 120)) | ((s >= 16) & (s < 24) & (i == s - 16))


def strip_match(i, j, f):
    s = j & 31
    west = (s >= 12) & (s < 16) & (i == 4 * f + s - 12)
    east = (s >= 8) & (s < 12) & (i == 4 * f + 4 + s - 8)
    return west | east


def tables_kernel(own_q, own, strip, back):
    one_hot(own_q, NTR * 128, 128, lambda i, j, r, c: own_match(i, j) & ((j >> 5) == r))
    one_hot(own, 128, 128, lambda i, j, r, c: own_match(i, j))

    def strips(i, j, odd, c):
        if c > 0:
            f = NTR + c - 1
            if f % 2 != odd:
                return i < 0
            return strip_match(i, j, f)
        hit = i < 0
        for f in range(odd, NTR, 2):
            hit |= strip_match(i, j, f) & ((j >> 5) == f)
        return hit

    one_hot(strip, strip.shape[0], strip.shape[1], strips)
    one_hot(
        back,
        128,
        NTR * 128,
        lambda i, j, r, c: (i == 32 * c + 16 + j) & (j < 4)
        | (i == 32 * c + 4 + j - 124) & (j >= 124),
    )


TABLES = [(NTR * 128, 128), (128, 128), (256, 5 * 128), (128, NTR * 128)]


def unit_place(n):
    return UNIT * (n // 4), 32 * (n % 4)


def strip_rows(count, rows):
    return UNIT * ((count * ((rows + 16) // UNIT) + 3) // 4)


def pack_columns(first, levels, x, lat, first_ref, second_ref, count):
    units = (x.shape[1] + 16) // UNIT
    lane = lane_ids(UNIT)
    west = east = jnp.zeros((UNIT, 128), jnp.float32)
    for l in range(count):
        level = first + l
        fields = range(FIELDS if level == 0 else FIELDS - 1)
        whole = []
        for f in fields:
            s, n = lat_halo_blocks(lat, f, level)
            whole.append(jnp.concatenate([s, x[field_index(f, level, levels)], n], axis=0))
        for r in range(units):
            place, base = unit_place(l * units + r)
            for f in fields:
                at = base + 4 * f
                turned = pltpu.roll(whole[f][UNIT * r : UNIT * r + UNIT], (at - 124) % 128, 1)
                east = jnp.where((lane >= at) & (lane < at + 4), turned, east)
                to = (at + 4) % 128
                west = jnp.where((lane >= to) & (lane < to + 4), turned, west)
            if base == 96 or (l == count - 1 and r == units - 1):
                here = slice(place, place + UNIT)
                first_ref[here], second_ref[here] = pick(parity("gx"), east, west)
                west = east = jnp.zeros((UNIT, 128), jnp.float32)


def fetch_kernel(after, t, v, m, o, w, x, out, mask, sems, sem):
    copies = tile_copies(t.shape[1], t, v, m, o, x, mask, sems)
    copies.append(pltpu.make_async_copy(w.at[pl.ds(0, out.shape[0])], out, sem))
    for copy in copies:
        copy.start()
    finish_tile(copies[:-1], x, mask)
    copies[-1].wait()


def fetch(after, arrays, weights):
    levels, rows = arrays[0].shape[1:3]
    part = (rows * FIRST // 8,) + weights.shape[1:]
    return pl.pallas_call(
        fetch_kernel,
        in_specs=[pl.BlockSpec(memory_space=pl.ANY)]
        + [pl.BlockSpec(memory_space=pltpu.HBM)] * 5,
        out_specs=[WHOLE] * 2,
        out_shape=[
            pltpu.VMEM(tile_shape(levels, rows), jnp.float32),
            pltpu.VMEM(part, weights.dtype),
        ],
        scratch_shapes=[
            pltpu.VMEM(arrays[3].shape, jnp.int32),
            pltpu.SemaphoreType.DMA((FIELDS,)),
            pltpu.SemaphoreType.DMA,
        ],
        compiler_params=pltpu.CompilerParams(vmem_limit_bytes=2 << 20),
        cost_estimate=took(3),
        name="fetch",
    )(after, *(in_hbm(a) for a in (*arrays, weights)))


def lon_pack_kernel(levels, la, lb, x, first_ref, second_ref):
    pack_columns(0, levels, x, (la, lb), first_ref, second_ref, 1)


def others_pack_kernel(levels, skip, la, lb, x, w, first_ref, second_ref, *refs):
    out, own_q, own, strip, back, sem = refs
    copy = pltpu.make_async_copy(w.at[pl.ds(skip, out.shape[0])], out, sem)
    copy.start()
    pack_columns(1, levels, x, (la, lb), first_ref, second_ref, levels - 1)
    tables_kernel(own_q, own, strip, back)
    copy.wait()


def lon_pack(lat, tile, levels, weights=None):
    rows = tile.shape[1]
    count = levels - 1 if weights is not None else 1
    out = [jax.ShapeDtypeStruct((strip_rows(count, rows), 128), jnp.float32)] * 2
    if weights is None:
        kernel = functools.partial(lon_pack_kernel, levels)
    else:
        kernel = functools.partial(others_pack_kernel, levels, rows * FIRST // 8)
        out.append(pltpu.VMEM((rows * SECOND // 8,) + weights.shape[1:], weights.dtype))
        out += [pltpu.VMEM(shape, jnp.bfloat16) for shape in TABLES]
    more = [] if weights is None else [in_hbm(weights)]
    return pl.pallas_call(
        kernel,
        in_specs=[WHOLE] * 3 + [pl.BlockSpec(memory_space=pltpu.HBM)] * len(more),
        out_specs=[WHOLE] * len(out),
        out_shape=out,
        scratch_shapes=[pltpu.SemaphoreType.DMA] * len(more),
        compiler_params=pltpu.CompilerParams(vmem_limit_bytes=4 << 20),
        cost_estimate=took(0.3 if weights is None else 2),
        name="lon_pack",
    )(*lat, in_vmem(tile), *more)


def unpack_field(ext, f, level, levels, x, lat):
    rows = x.shape[1]
    s, n = lat_halo_blocks(lat, f, level)
    ext[OFF - 8 : OFF] = s
    ext[OFF : OFF + rows] = x[field_index(f, level, levels)]
    ext[OFF + rows : OFF + rows + 8] = n


def terms(x, count):
    out = []
    for i in range(count):
        out.append(x.astype(jnp.bfloat16))
        if i < count - 1:
            x = x - out[-1].astype(jnp.float32)
    return out


def moved(parts, table, count):
    n = parts[0].shape[0]
    split = [terms(p, count) for p in parts]
    lhs = jnp.concatenate(
        [jnp.concatenate([p[i] for p in split], axis=1) for i in range(count)], axis=0
    )
    out = jnp.dot(lhs, table, preferred_element_type=jnp.float32)
    total = out[:n]
    for i in range(1, count):
        total = total + out[i * n : i * n + n]
    return total


def strip_parts(lon, level, units):
    near = lane_ids(UNIT) % 8 < 4
    first, second, base = lon
    even, odd = [], []
    for r in range(units):
        row, lane = level_unit(level - base, r, units)
        here = pl.ds(row, UNIT)
        e, w = pick(parity("gx"), first[here, :], second[here, :])
        even.append(pltpu.roll(jnp.where(near, w, e), (128 - lane) & 127, 1))
        odd.append(pltpu.roll(jnp.where(near, e, w), (128 - lane) & 127, 1))
    return [jnp.concatenate(even, axis=0), jnp.concatenate(odd, axis=0)]


def level_unit(l, r, units):
    n = l * units + r
    if isinstance(n, int):
        return unit_place(n)
    return pl.multiple_of(UNIT * (n >> 2), UNIT), 32 * (n & 3)


def side_arrays(rows, level, fields, sides, columns, lon, own, strip, count):
    body = slice(OFF - 8, OFF + rows + 8)
    packed = strip_parts(lon, level, (rows + 16) // UNIT)
    first, last = 128 * columns[0], 128 * (columns[-1] + 1)
    got = moved(packed, strip[:, first:last], count)
    for i, (parts, side, table) in enumerate(zip(fields, sides, own)):
        mine = moved([p[body] for p in parts], table[...], count)
        side[body] = mine + got[:, 128 * i : 128 * i + 128]


def to_right(a):
    return pltpu.roll(a, 127, 1)


def to_left(a):
    return pltpu.roll(a, 1, 1)


def chunks(first, last, size):
    return [slice(r, r + size) for r in range(first, last, size)]


def around(rows):
    return chunks(OFF - 8, OFF + rows + 8, 24)


def moved_rows(here, by):
    return slice(here.start + by, here.stop + by)


def open_faces(rows, ocean, east, north):
    for here in around(rows):
        o = ocean[here]
        east[here] = 0.5 * (o * to_right(o))
        north[here] = 0.5 * (o * ocean[moved_rows(here, 1)])


def faces(a, b, mix, face):
    vel = a + b
    low = jnp.maximum(vel, 0.0) + mix
    return face * low, face * (low - vel)


def coefficients(rows, u, v, k, east, north, coef, above):
    for here in around(rows):
        up = moved_rows(here, 1)
        a, b = faces(v[here], v[up], k[here] + k[up], north[here])
        above[here] = a
        coef[3, here] = b
    for here in around(rows):
        below = moved_rows(here, -1)
        us, ks = u[here], k[here]
        a, b = faces(us, to_right(us), ks + to_right(ks), east[here])
        wa, wb = to_left(a), to_left(b)
        south = above[below]
        coef[0, here] = (1.0 - (a + wb)) - (above[here] + coef[3, below])
        coef[1, here] = b
        coef[2, here] = wa
        coef[4, here] = south


def stencil(c, q, here):
    mid = q[here]
    return (
        c[0] * mid
        + c[1] * to_right(mid)
        + c[2] * to_left(mid)
        + c[3] * q[moved_rows(here, 1)]
        + c[4] * q[moved_rows(here, -1)]
    )


def advance(rows, coef, side_coef, q, side):
    for step in range(STEPS):
        src, dst = step % 2, (step + 1) % 2
        last = step == STEPS - 1
        for here in chunks(OFF, OFF + rows, 32) if last else around(rows):
            c = [side_coef[i, here] for i in range(5)]
            side[dst, here] = stencil(c, side.at[src], here)
            c = [coef[i, here] for i in range(5)]
            for i in range(NTR):
                q[dst, i, here] = stencil(c, q.at[src, i], here)


def field_scratch(rows):
    ext = (rows + 32, 128)
    return [
        pltpu.VMEM((count,) + ext, jnp.float32)
        for count in (3, 3, 4, 2, 5, 5)
    ] + [
        pltpu.VMEM((2, NTR) + ext, jnp.float32),
        pltpu.VMEM((2,) + ext, jnp.float32),
    ]


def set_faces(x, levels, lat, lon, tables, scratch):
    rows = x.shape[1]
    own_q, own, strip, back = tables
    vel, side_vel, face = scratch[:3]
    ocean, side = vel.at[0], side_vel.at[0]
    unpack_field(ocean, FIELDS - 1, 0, levels, x, lat)
    side_arrays(rows, 0, [[ocean]], [side], [NTR], lon, [own], strip, 1)
    open_faces(rows, ocean, face.at[0], face.at[1])
    open_faces(rows, side, face.at[2], face.at[3])


def run_level(level, x, levels, lat, lon, tables, scratch, count):
    rows = x.shape[1]
    own_q, own, strip, back = tables
    vel, side_vel, face, above, coef, side_coef, q, side = scratch
    now = [q.at[0, i] for i in range(NTR)]
    three = [vel.at[i] for i in range(3)]
    for i, ref in enumerate(now + three):
        unpack_field(ref, i, level, levels, x, lat)
    side_arrays(
        rows,
        level,
        [now] + [[ref] for ref in three],
        [side.at[0]] + [side_vel.at[i] for i in range(3)],
        range(NTR),
        lon,
        [own_q, own, own, own],
        strip,
        count,
    )
    coefficients(rows, *three, face.at[0], face.at[1], coef, above.at[0])
    coefficients(
        rows, *(side_vel.at[i] for i in range(3)), face.at[2], face.at[3], side_coef, above.at[1]
    )
    advance(rows, coef, side_coef, q, side)
    body = slice(OFF, OFF + rows)
    ends = moved([side[0, body]], back[...], count)
    lane = lane_ids(rows)
    inner = (lane >= STEPS) & (lane < 128 - STEPS)
    return [
        jnp.where(inner, q[0, i, body], ends[:, 128 * i : 128 * i + 128]) for i in range(NTR)
    ]


def surface_kernel(order, accs, levels, slot, x, la, lb, wa, wb, *refs):
    tables, w_held, w_more, w_hbm = refs[:4], refs[4], refs[5], refs[6]
    out_q, out_send, out_keep = refs[7:10]
    scratch, surf, w_last, sem, sums = refs[10:18], refs[18], refs[19], refs[20], refs[21:]
    rows = x.shape[1]
    done_rows = w_held.shape[0] + w_more.shape[0]
    copy = pltpu.make_async_copy(w_hbm.at[pl.ds(done_rows, w_last.shape[0])], w_last, sem)
    copy.start()
    lat, lon = (la, lb), (wa, wb, 0)
    set_faces(x, levels, lat, lon, tables, scratch)
    ocean = x[field_index(FIELDS - 1, 0, levels)]
    for i, done in enumerate(run_level(0, x, levels, lat, lon, tables, scratch, 3)):
        out_q[i] = done
        surf[pl.ds(i, rows, stride=8), :] = done * ocean
    surf[pl.ds(NTR, rows, stride=8), :] = ocean
    for i in range(NTR + 1, 8):
        surf[pl.ds(i, rows, stride=8), :] = jnp.zeros((rows, 128), jnp.float32)
    for d in sums:
        d[...] = jnp.zeros_like(d)
    first = sub_ids(16) < 8
    kb = w_held.shape[1]

    def body(w, base, j, carry):
        i = j + base
        s = surf[pl.ds(pl.multiple_of(16 * i, 16), 16), :]
        lhs = jnp.concatenate(
            [jnp.where(first, s, 0.0), jnp.where(first, 0.0, s)], axis=1
        ).astype(jnp.bfloat16)
        for k in range(0, kb, 2):
            rhs = jnp.concatenate(
                [
                    jnp.concatenate([w[2 * j + r, k], w[2 * j + r, k + 1]], axis=1)
                    for r in range(2)
                ],
                axis=0,
            )
            part = jnp.dot(lhs, rhs, preferred_element_type=jnp.float32)
            for r in range(2):
                for kk in range(2):
                    d = sums[(k + kk) % accs]
                    at = pl.ds(
                        pl.multiple_of(8 * slot[k + kk, 2 * i + r], 8), 8
                    )
                    d[at, :] += part[8 * r : 8 * r + 8, 128 * kk : 128 * kk + 128]
        return carry

    start = 0
    for w in (w_held, w_more, w_last):
        if w is w_last:
            copy.wait()
        pairs = w.shape[0] // 2
        lax.fori_loop(0, pairs, functools.partial(body, w, start), 0, unroll=16)
        start += pairs
    chunk = ABD * (NTR + 1)
    half = len(order) // 2
    for place, owner in enumerate(order):
        ref, base = (out_keep, place) if place < half else (out_send, place - half)
        for f in range(NTR + 1):
            total = sums[0][pl.ds(owner * ABD * 8 + f, ABD, stride=8), :]
            for d in sums[1:]:
                total = total + d[pl.ds(owner * ABD * 8 + f, ABD, stride=8), :]
            at = base * chunk + f * ABD
            ref[at : at + ABD, :] = total


def surface(order, slot, tile, levels, lat, lon, tables, held, weights):
    rows = tile.shape[1]
    owners = len(order)
    accs = 2 if owners <= 32 else 1
    half = owners // 2 * ABD * (NTR + 1)
    last = (rows - sum(w.shape[0] for w in held),) + weights.shape[1:]
    return pl.pallas_call(
        functools.partial(surface_kernel, order, accs, levels),
        in_specs=[SCALARS] + [WHOLE] * 11 + [pl.BlockSpec(memory_space=pltpu.HBM)],
        out_specs=[WHOLE] * 3,
        scratch_shapes=field_scratch(rows)
        + [pltpu.VMEM((rows * 8 + 8, 128), jnp.float32)]
        + [pltpu.VMEM(last, weights.dtype), pltpu.SemaphoreType.DMA]
        + [pltpu.VMEM((owners * ABD * 8 + 8, 128), jnp.float32)] * accs,
        out_shape=[
            jax.ShapeDtypeStruct((NTR, rows, 128), jnp.float32),
            jax.ShapeDtypeStruct((half, 128), jnp.float32),
            jax.ShapeDtypeStruct((half, 128), jnp.float32),
        ],
        compiler_params=pltpu.CompilerParams(vmem_limit_bytes=24 << 20),
        cost_estimate=took(7),
        name="surface",
    )(slot, in_vmem(tile), *lat, *lon, *tables, *(in_vmem(w) for w in held), in_hbm(weights))


def deep_kernel(first, levels, x, la, lb, oa, ob, wa, wb, *refs):
    tables, base, out, scratch = refs[:4], refs[4], refs[5], refs[6:]
    lat = (la, lb)
    level = pl.program_id(0) + first

    @pl.when(pl.program_id(0) == 0)
    def _():
        set_faces(x, levels, lat, (oa, ob, 0), tables, scratch)

    if first == 0:
        @pl.when(level == 0)
        def _():
            out[:, 0] = base[...]

    @pl.when(level > 0)
    def _():
        lon = (wa, wb, 1)
        for i, done in enumerate(run_level(level, x, levels, lat, lon, tables, scratch, COUNT)):
            out[i, 0] = done


def deep(tile, levels, lat, lon0, lon, tables, base, first, count):
    rows = tile.shape[1]
    return pl.pallas_call(
        functools.partial(deep_kernel, first, levels),
        grid=(count,),
        in_specs=[WHOLE] * 11 + [pl.BlockSpec(memory_space=pl.ANY) if first else WHOLE],
        out_specs=pl.BlockSpec((NTR, 1, rows, 128), lambda l: (0, l + first, 0, 0)),
        out_shape=jax.ShapeDtypeStruct((NTR, levels, rows, 128), jnp.float32),
        scratch_shapes=field_scratch(rows),
        input_output_aliases={11: 0} if first else {},
        compiler_params=pltpu.CompilerParams(vmem_limit_bytes=16 << 20),
        cost_estimate=took(1.3 * count),
        name="deep",
    )(in_vmem(tile), *lat, *lon0, *lon, *tables, base)


def swap(first, second, axis, ring):
    n = lax.axis_size(axis)
    even = [(i, i + 1) for i in range(0, n - 1, 2)]
    odd = [(i, (i + 1) % n) for i in range(1, n if ring else n - 1, 2)]
    second = lax.ppermute(second, axis, odd + [(j, i) for i, j in odd])
    first = lax.ppermute(first, axis, even + [(j, i) for i, j in even])
    return first, second


def partner(a, mask, n):
    return lax.ppermute(a, AXES, [(i, i ^ mask) for i in range(n)])


def rounds_of(owners):
    bits = owners.bit_length() - 1
    out, at = [(0, 1)], 1
    while at < bits:
        width = min(2, bits - at)
        out.append((at, width))
        at += width
    return out


def cuts(levels, rounds):
    between = [2 + (levels - 4) * i // (rounds - 2) for i in range(rounds - 1)]
    return [0] + between + [levels]


def order_of(owners):
    def key(owner):
        return tuple((-(owner >> at)) & ((1 << width) - 1) for at, width in rounds_of(owners))
    return sorted(range(owners), key=key)


def per_device(tracers, velocity, mixing, land_mask, remap_weights, remap_dest):
    owners = lax.axis_size("gx") * lax.axis_size("gy")
    levels = tracers.shape[1]
    me = lax.axis_index("gx") * lax.axis_size("gy") + lax.axis_index("gy")
    dest = remap_dest[:, 0].T
    slot = jnp.bitwise_xor(dest // ABD, me) * ABD + dest % ABD

    arrays = (tracers, velocity, mixing, land_mask)
    strips = lat_pack(*arrays)
    lat = swap(*strips, "gy", False)
    slot, first = lax.optimization_barrier((slot, strips[0]))
    tile, held = fetch(slot, arrays, remap_weights)
    lat, tile, held = lax.optimization_barrier((lat, tile, held))
    first, second = lon_pack(lat, tile, levels)
    lon0 = swap(first, second, "gx", True)
    lat, first = lax.optimization_barrier((lat, first))
    first, second, more, *tables = lon_pack(lat, tile, levels, remap_weights)
    lon0, first, more, tables = lax.optimization_barrier((lon0, first, more, tables))
    lon = swap(first, second, "gx", True)

    order = order_of(owners)
    done, send, keep = surface(
        order, slot, tile, levels, lat, lon0, tables, (held, more), remap_weights
    )
    lon, send = lax.optimization_barrier((lon, send))
    rounds = rounds_of(owners)
    cut = cuts(levels, len(rounds))
    parts = [keep, send]
    values = done
    for i, (at, width) in enumerate(rounds):
        got = [partner(parts[j], (-j % (1 << width)) << at, owners) for j in range(1, 1 << width)]
        values = deep(tile, levels, lat, lon0, lon, tables, values, cut[i], cut[i + 1] - cut[i])
        got, values = lax.optimization_barrier((got, values))
        total = parts[0]
        for g in got:
            total = total + g
        if i < len(rounds) - 1:
            lon, total = lax.optimization_barrier((lon, total))
            parts = total.reshape((1 << rounds[i + 1][1], -1, 128))
    atmo = total.reshape(NTR + 1, ABD, 128).transpose(1, 0, 2)
    return values, atmo


def solution(mesh):
    placed = (
        P(None, None, "gy", "gx"),
        P(None, None, "gy", "gx"),
        P(None, "gy", "gx"),
        P("gy", "gx"),
        P("gy", None, "gx", None),
        P("gy", "gx", None),
    )
    return jax.shard_map(
        per_device,
        mesh=mesh,
        in_specs=placed,
        out_specs=(P(None, None, "gy", "gx"), P(("gx", "gy"), None, None)),
        check_vma=False,
    )
```
